32 devices in a mesh: merge: 4 (over z), row: 4 (over x, core), col: 2 (over y).
Axes of the slice: x: 2, y: 2, z: 4, core: 2. Of those that a mesh axis runs over, the one named last changes fastest.
Arguments:
- eigen_rows: bfloat16 [4, 128, 16384], P('merge', 'row', 'col'), may hold values from -6 to 6
- live_one: int32 [4], replicated, may hold values from 2048 to 6144, as said below
- order_one: int32 [4, 16384], P('merge'), may hold values from 0 to 16383, each once within a row
- poles_one: float32 [4, 16384], P('merge'), may hold values from -2048 to 2048.3, as said below
- weights_one: float32 [4, 16384], P('merge'), may hold values from 0.003 to 32, as said below
- roots_one: float32 [4, 16384], P('merge'), may hold values from -2047.55 to 2048.85, as said below
- live_two: int32 [4], replicated, may hold values from 2048 to 6144, as said below
- order_two: int32 [4, 16384], P('merge'), may hold values from 0 to 16383, each once within a row
- poles_two: float32 [4, 16384], P('merge'), may hold values from -2048 to 2048.3, as said below
- weights_two: float32 [4, 16384], P('merge'), may hold values from 0.003 to 32, as said below
- roots_two: float32 [4, 16384], P('merge'), may hold values from -2047.55 to 2048.85, as said below
Outputs:
- vectors_two: bfloat16 [4, 128, 32768], P('merge', 'row', 'col')
The draws below stay inside these ranges and needn't reach their ends.
Inputs may be any that keep to these rules, and one draw needn't show every extreme that they name: `live_one`: both ends of the range are reached in every draw. `live_two`: both ends of the range are reached in every draw. `weights_one`: Positive. `weights_two`: Positive. `poles_one`: every offset minus its floor lies in [0, 0.3]. `roots_one`: every offset minus its floor lies in [0.45, 0.85], so every root stays 0.15 or more from every pole. `poles_two`: every offset minus its floor lies in [0, 0.3]. `roots_two`: every offset minus its floor lies in [0.45, 0.85], so every root stays 0.15 or more from every pole.
All inputs are finite; a program needn't handle non-finite values.
Results may differ from the reference program's by a relative error of at most 0.0031.
Values may be sent and summed in bfloat16 or wider, within the bound.
A program may use at most 64 MiB of HBM per device.

```python
import math
import jax
import jax.numpy as jnp
from jax import lax

MERGE_ORDER = 16384
ROWS = 128
N_MERGE = 4


def count_law(key):
    first_key, second_key, third_key = jax.random.split(key, 3)
    counts = jax.random.randint(first_key, (N_MERGE,), MERGE_ORDER // 8, 3 * MERGE_ORDER // 8 + 1)
    highest = jax.random.randint(second_key, (), 0, N_MERGE)
    lowest = (highest + 1 + jax.random.randint(third_key, (), 0, N_MERGE - 1)) % N_MERGE
    numbers = jnp.arange(N_MERGE)
    counts = jnp.where(numbers == highest, 3 * MERGE_ORDER // 8, counts)
    counts = jnp.where(numbers == lowest, MERGE_ORDER // 8, counts)
    return counts.astype(jnp.int32)


def weight_law(key):
    scale_key, phase_key = jax.random.split(key)
    scaled = jnp.exp(jax.random.uniform(scale_key, (N_MERGE, MERGE_ORDER), jnp.float32, math.log(0.1), 0.0))
    phases = jax.random.uniform(phase_key, (N_MERGE, 1), jnp.float32, 0.0, 2.0 * math.pi)
    slots = jnp.arange(MERGE_ORDER).astype(jnp.float32)
    swing = 0.5
    period = 1024.0
    return scaled * jnp.exp(math.log(10.0) * swing * jnp.sin(2.0 * math.pi * slots / period + phases))


def offset_law(key, lowest, highest):
    fraction_key = jax.random.fold_in(key, 0)
    fraction = jax.random.uniform(fraction_key, (N_MERGE, MERGE_ORDER), jnp.float32, lowest, highest)
    return fraction


def draw_live_one(key, part):
    return count_law(jax.random.fold_in(key, 11))


def draw_live_two(key, part):
    return count_law(jax.random.fold_in(key, 23))


def draw_weights_one(key, part):
    return weight_law(jax.random.fold_in(key, 37))


def draw_weights_two(key, part):
    return weight_law(jax.random.fold_in(key, 41))


def draw_poles_one(key, part):
    return offset_law(jax.random.fold_in(key, 53), 0.0, 0.3)


def draw_roots_one(key, part):
    return offset_law(jax.random.fold_in(key, 59), 0.45, 0.85)


def draw_poles_two(key, part):
    return offset_law(jax.random.fold_in(key, 61), 0.0, 0.3)


def draw_roots_two(key, part):
    return offset_law(jax.random.fold_in(key, 67), 0.45, 0.85)


def block_scale(own_key, shape, cuts, smallest, top_value):
    factor_of = 1.0
    for axis_at, parts in cuts:
        draws = jax.random.uniform(jax.random.fold_in(jax.random.fold_in(own_key, 6), axis_at), (parts,), jnp.float32, smallest / len(cuts), top_value / len(cuts))
        factor_of = factor_of * jnp.repeat(jnp.exp(draws), shape[axis_at] // parts).reshape((-1,) + (1,) * (len(shape) - 1 - axis_at))
    return factor_of


def centred(stream_key, shape, scale, limit, cuts=(), kind=jnp.bfloat16):
    values = scale * jax.random.normal(stream_key, shape, jnp.float32)
    if cuts:
        values = values * block_scale(stream_key, shape, cuts, -0.22, 0.18)
    return jnp.clip(values, -limit, limit).astype(kind)


def setup_inputs(seed: int = 0) -> dict:
    streams_of = jax.random.split(jax.random.key(seed), 12)
    eigen_rows = centred(streams_of[0], (N_MERGE, ROWS, MERGE_ORDER), 1.0, 6.0, ((0, 4), (1, 4), (2, 2)))
    live_one = draw_live_one(jax.random.fold_in(streams_of[11], 71), 0)
    order_one = jax.vmap(lambda own: jax.random.permutation(own, MERGE_ORDER))(jax.random.split(streams_of[2], N_MERGE)).reshape((N_MERGE, MERGE_ORDER)).astype(jnp.int32)
    poles_one = draw_poles_one(jax.random.fold_in(streams_of[11], 71), 0)
    weights_one = draw_weights_one(jax.random.fold_in(streams_of[11], 71), 0)
    roots_one = draw_roots_one(jax.random.fold_in(streams_of[11], 71), 0)
    live_two = draw_live_two(jax.random.fold_in(streams_of[11], 71), 0)
    order_two = jax.vmap(lambda own: jax.random.permutation(own, MERGE_ORDER))(jax.random.split(streams_of[7], N_MERGE)).reshape((N_MERGE, MERGE_ORDER)).astype(jnp.int32)
    poles_two = draw_poles_two(jax.random.fold_in(streams_of[11], 71), 0)
    weights_two = draw_weights_two(jax.random.fold_in(streams_of[11], 71), 0)
    roots_two = draw_roots_two(jax.random.fold_in(streams_of[11], 71), 0)
    return {"eigen_rows": eigen_rows, "live_one": live_one, "order_one": order_one, "poles_one": poles_one, "weights_one": weights_one, "roots_one": roots_one, "live_two": live_two, "order_two": order_two, "poles_two": poles_two, "weights_two": weights_two, "roots_two": roots_two}


column_block = 512

def square_sums(source_place, source_shift, source_weight, live_rows, column_place, column_shift):
    numbers = jnp.arange(source_place.shape[0], dtype=jnp.int32)
    squares = jnp.where(numbers < live_rows, source_weight * source_weight, 0.0)

    def one_block(pieces):
        places, shifts = pieces
        distance = source_place[:, None] - places[None, :] + (source_shift[:, None] - shifts[None, :])
        return lax.optimization_barrier(jnp.sum(squares[:, None] / (distance * distance), axis=0))
    blocks = lax.map(one_block, (column_place.reshape(-1, column_block), column_shift.reshape(-1, column_block)))
    return blocks.reshape(-1)

def apply_cauchy(permuted, source_place, source_shift, source_weight, live_rows, column_place, column_shift, inverse_norm, live_columns):
    numbers = jnp.arange(source_place.shape[0], dtype=jnp.int32)
    row_keep = numbers < live_rows
    columns = jnp.arange(column_place.shape[0], dtype=jnp.int32)

    def one_block(pieces):
        places, shifts, inverse, indices = pieces
        distance = source_place[:, None] - places[None, :] + (source_shift[:, None] - shifts[None, :])
        entries = source_weight[:, None] / distance * inverse[None, :]
        entries = jnp.where(row_keep[:, None] & (indices < live_columns)[None, :], entries, 0.0)
        rounded = lax.optimization_barrier(entries.astype(jnp.bfloat16)).astype(jnp.float32)
        return jnp.dot(permuted, rounded, precision=lax.Precision.HIGHEST)
    blocks = lax.map(one_block, (column_place.reshape(-1, column_block), column_shift.reshape(-1, column_block), inverse_norm.reshape(-1, column_block), columns.reshape(-1, column_block)))
    return jnp.transpose(blocks, (1, 0, 2)).reshape(permuted.shape[0], -1)

def reference(eigen_rows, live_one, order_one, poles_one, weights_one, roots_one, live_two, order_two, poles_two, weights_two, roots_two):
    merge_order = order_one.shape[1]
    slots = jnp.arange(merge_order, dtype=jnp.int32)
    level_list = []
    for merge_number in range(N_MERGE):
        live_level = live_one[merge_number]
        permuted = jnp.take(eigen_rows[merge_number].astype(jnp.float32), order_one[merge_number], axis=1)
        places = slots.astype(jnp.float32)
        sums = square_sums(places, poles_one[merge_number], weights_one[merge_number], live_level, places, roots_one[merge_number])
        inverse = 1.0 / jnp.sqrt(sums)
        cauchy = apply_cauchy(permuted, places, poles_one[merge_number], weights_one[merge_number], live_level, places, roots_one[merge_number], inverse, live_level)
        level_list.append(jnp.where(slots[None, :] < live_level, cauchy, permuted).astype(jnp.bfloat16))
    columns = jnp.arange(2 * merge_order, dtype=jnp.int32)
    outputs = []
    for pair_number in range(N_MERGE // 2):
        first_merge = 2 * pair_number
        second_merge = first_merge + 1
        count_first = live_two[first_merge]
        count_second = live_two[second_merge]
        joined = count_first + count_second
        from_first = columns < count_first
        slot_index = jnp.clip(jnp.where(from_first, columns, columns - count_first), 0, merge_order - 1)
        column_place = (2 * slot_index + jnp.where(from_first, 0, 1)).astype(jnp.float32)
        column_shift = jnp.where(from_first, jnp.take(roots_two[first_merge], slot_index), jnp.take(roots_two[second_merge], slot_index))
        sums = square_sums((2 * slots).astype(jnp.float32), poles_two[first_merge], weights_two[first_merge], count_first, column_place, column_shift)
        sums = sums + square_sums((2 * slots + 1).astype(jnp.float32), poles_two[second_merge], weights_two[second_merge], count_second, column_place, column_shift)
        inverse = 1.0 / jnp.sqrt(sums)
        for half_index in range(2):
            merge_number = first_merge + half_index
            permuted = jnp.take(level_list[merge_number].astype(jnp.float32), order_two[merge_number], axis=1)
            cauchy = apply_cauchy(permuted, (2 * slots + half_index).astype(jnp.float32), poles_two[merge_number], weights_two[merge_number], live_two[merge_number], column_place, column_shift, inverse, joined)
            extra = columns - joined
            first_source = extra < merge_order - count_first
            if half_index == 0:
                own_source = first_source
                position = count_first + extra
            else:
                own_source = jnp.logical_not(first_source)
                position = count_second + extra - (merge_order - count_first)
            position = jnp.clip(position, 0, merge_order - 1).astype(jnp.int32)
            moved = jnp.where(own_source[None, :], jnp.take(permuted, position, axis=1), 0.0)
            outputs.append(jnp.where(columns[None, :] < joined, cauchy, moved).astype(jnp.bfloat16))
    return jnp.stack(outputs)
```

```python
import functools

import jax
import jax.numpy as jnp
from jax import lax
from jax.experimental import pallas as pl
from jax.experimental.pallas import tpu as pltpu
from jax.sharding import PartitionSpec as P

LANE = 128
POLE_TILE = 256
VMEM_LIMIT = 56 * 1024 * 1024


def inverse_of(distance):
    guess = pl.reciprocal(distance, approx=True)
    return guess * (2.0 - distance * guess)


def spec(space):
    return pl.BlockSpec(memory_space=space)


def fill_table(source_ref, table_ref, start):
    rows, width = source_ref.shape
    blocks = width // LANE

    def one(step, carry):
        opening = pl.multiple_of(step * LANE, LANE)
        block = source_ref[:, pl.ds(opening, LANE)].astype(jnp.float32)
        table_ref[pl.ds(pl.multiple_of(start + opening, LANE), LANE), 0:rows] = block.T
        return carry

    lax.fori_loop(0, blocks, one, 0)


def pick_block(table_ref, stage_ref, index_of, rows):
    def eight(turn, carry):
        base = turn * 16
        for k in range(16):
            stage_ref[pl.ds(base + k, 1), 0:rows] = table_ref[pl.ds(index_of(base + k), 1), 0:rows]
        return carry

    lax.fori_loop(0, LANE // 16, eight, 0)
    return stage_ref[...].T[0:rows, :].astype(jnp.bfloat16)


def pick_one_kernel(info_ref, order_ref, source_ref, out_ref, table_ref, stage_ref):
    rows = source_ref.shape[0]
    fill_table(source_ref, table_ref, 0)
    stage_ref[...] = jnp.zeros(stage_ref.shape, jnp.float32)
    out_ref[...] = jnp.zeros(out_ref.shape, out_ref.dtype)
    first, live = info_ref[0], info_ref[1]
    count = jnp.clip((live - first + LANE - 1) // LANE, 0, out_ref.shape[1] // LANE)

    def one(step, carry):
        opening = pl.multiple_of(step * LANE, LANE)
        out_ref[:, pl.ds(opening, LANE)] = pick_block(
            table_ref, stage_ref, lambda k: order_ref[first + opening + k], rows
        )
        return carry

    lax.fori_loop(0, count, one, 0)


def pick_one(info, order, source, width):
    rows, total = source.shape
    return pl.pallas_call(
        pick_one_kernel,
        out_shape=jax.ShapeDtypeStruct((rows, width), jnp.bfloat16),
        in_specs=[spec(pltpu.SMEM), spec(pltpu.SMEM), spec(pltpu.VMEM)],
        out_specs=spec(pltpu.VMEM),
        scratch_shapes=[
            pltpu.VMEM((total, LANE), jnp.float32),
            pltpu.VMEM((LANE, LANE), jnp.float32),
        ],
        compiler_params=pltpu.CompilerParams(vmem_limit_bytes=VMEM_LIMIT),
    )(info, order, source)


def pick_two_kernel(
    info_ref, order_ref, place_ref, level_ref, source_ref, out_ref, moved_ref, table_ref, stage_ref
):
    rows = source_ref.shape[0]
    total = order_ref.shape[0]
    fill_table(level_ref, table_ref, 0)
    fill_table(source_ref, table_ref, level_ref.shape[1])
    stage_ref[...] = jnp.zeros(stage_ref.shape, jnp.float32)
    out_ref[...] = jnp.zeros(out_ref.shape, out_ref.dtype)
    moved_ref[...] = jnp.zeros(moved_ref.shape, moved_ref.dtype)
    first, live = info_ref[0], info_ref[1]
    count = jnp.clip((live - first + LANE - 1) // LANE, 0, out_ref.shape[1] // LANE)

    def one(step, carry):
        opening = pl.multiple_of(step * LANE, LANE)
        out_ref[:, pl.ds(opening, LANE)] = pick_block(
            table_ref, stage_ref, lambda k: place_ref[order_ref[first + opening + k]], rows
        )
        return carry

    lax.fori_loop(0, count, one, 0)
    offset, low, high = info_ref[2], info_ref[3], info_ref[4]

    def other(step, carry):
        opening = pl.multiple_of(step * LANE, LANE)
        moved_ref[:, pl.ds(opening, LANE)] = pick_block(
            table_ref,
            stage_ref,
            lambda k: place_ref[order_ref[jnp.clip(opening + k + offset, 0, total - 1)]],
            rows,
        )
        return carry

    lax.fori_loop(low // LANE, (high + LANE - 1) // LANE, other, 0)


def pick_two(info, order, place, level, source, width, moved_width):
    rows, total = source.shape
    return pl.pallas_call(
        pick_two_kernel,
        out_shape=(
            jax.ShapeDtypeStruct((rows, width), jnp.bfloat16),
            jax.ShapeDtypeStruct((rows, moved_width), jnp.bfloat16),
        ),
        in_specs=[spec(pltpu.SMEM)] * 3 + [spec(pltpu.VMEM)] * 2,
        out_specs=(spec(pltpu.VMEM), spec(pltpu.VMEM)),
        scratch_shapes=[
            pltpu.VMEM((total + level.shape[1], LANE), jnp.float32),
            pltpu.VMEM((LANE, LANE), jnp.float32),
        ],
        compiler_params=pltpu.CompilerParams(vmem_limit_bytes=VMEM_LIMIT),
    )(info, order, place, level, source)


def distances(base, stride, half, shifts, column_place, column_shift):
    rows = shifts.shape[0]
    slot = lax.broadcasted_iota(jnp.int32, (rows, LANE), 0) + base
    place = (slot * stride + half).astype(jnp.float32)
    return (place - column_place) + (shifts - column_shift)


def norm_kernel(stride, info_ref, shift_ref, weight_ref, place_ref, root_ref, out_ref):
    live, half, blocks = info_ref[0], info_ref[1], info_ref[2]
    tiles = (live + POLE_TILE - 1) // POLE_TILE
    out_ref[...] = jnp.ones(out_ref.shape, jnp.float32)

    def one_block(block, carry):
        place = place_ref[pl.ds(block, 1), :]
        root = root_ref[pl.ds(block, 1), :]

        def one_tile(tile, running):
            opening = pl.multiple_of(tile * POLE_TILE, POLE_TILE)
            for part in range(POLE_TILE // 64):
                start = opening + part * 64
                distance = distances(
                    start, stride, half, shift_ref[pl.ds(start, 64), :], place, root
                )
                term = weight_ref[pl.ds(start, 64), :] * inverse_of(distance)
                running = running + jnp.sum((term * term).reshape(8, 8, LANE), axis=0)
            return running

        sums = lax.fori_loop(0, tiles, one_tile, jnp.zeros((8, LANE), jnp.float32))
        out_ref[pl.ds(block, 1), :] = jnp.sum(sums, axis=0, keepdims=True)
        return carry

    lax.fori_loop(0, blocks, one_block, 0)


def column_norms(stride, info, shift, weight, place, root):
    return pl.pallas_call(
        functools.partial(norm_kernel, stride),
        out_shape=jax.ShapeDtypeStruct(place.shape, jnp.float32),
        in_specs=[spec(pltpu.SMEM)] + [spec(pltpu.VMEM)] * 4,
        out_specs=spec(pltpu.VMEM),
        compiler_params=pltpu.CompilerParams(vmem_limit_bytes=VMEM_LIMIT),
    )(info, shift, weight, place, root)


def apply_kernel(
    stride, info_ref, rows_ref, shift_ref, weight_ref, place_ref, root_ref, inverse_ref, out_ref
):
    live, half, blocks = info_ref[0], info_ref[1], info_ref[2]
    tiles = (live + POLE_TILE - 1) // POLE_TILE
    row_total = rows_ref.shape[0]
    out_ref[...] = jnp.zeros(out_ref.shape, out_ref.dtype)

    def one_block(block, carry):
        place = place_ref[pl.ds(block, 1), :]
        root = root_ref[pl.ds(block, 1), :]
        inverse = inverse_ref[pl.ds(block, 1), :]

        def one_tile(tile, running):
            opening = pl.multiple_of(tile * POLE_TILE, POLE_TILE)
            pieces = []
            for part in range(POLE_TILE // 64):
                start = opening + part * 64
                distance = distances(
                    start, stride, half, shift_ref[pl.ds(start, 64), :], place, root
                )
                term = weight_ref[pl.ds(start, 64), :] * inverse_of(distance)
                pieces.append((term * inverse).astype(jnp.bfloat16))
            return running + jnp.dot(
                rows_ref[:, pl.ds(opening, POLE_TILE)],
                jnp.concatenate(pieces, axis=0),
                preferred_element_type=jnp.float32,
            )

        total = lax.fori_loop(0, tiles, one_tile, jnp.zeros((row_total, LANE), jnp.float32))
        out_ref[:, pl.ds(pl.multiple_of(block * LANE, LANE), LANE)] = total.astype(out_ref.dtype)
        return carry

    lax.fori_loop(0, blocks, one_block, 0)


def cauchy_product(stride, info, rows, shift, weight, place, root, inverse):
    return pl.pallas_call(
        functools.partial(apply_kernel, stride),
        out_shape=jax.ShapeDtypeStruct((rows.shape[0], place.size), jnp.bfloat16),
        in_specs=[spec(pltpu.SMEM)] + [spec(pltpu.VMEM)] * 6,
        out_specs=spec(pltpu.VMEM),
        compiler_params=pltpu.CompilerParams(vmem_limit_bytes=VMEM_LIMIT),
    )(info, rows, shift, weight, place, root, inverse)


def ceil_to(value, unit):
    return (value + unit - 1) // unit * unit


def own_blocks(values, group, member):
    spread = values.reshape(-1, group, LANE)
    return lax.dynamic_index_in_dim(spread, member, 1, keepdims=False)


def block_share(live, group, member):
    total = (live + LANE - 1) // LANE
    return jnp.maximum((total - member + group - 1) // group, 0)


def join_rows(piece):
    rows, width = piece.shape
    row_count, col_count = lax.axis_size("row"), lax.axis_size("col")
    parts = lax.all_gather(piece, ("row", "col"), axis=0, tiled=False)
    parts = parts.reshape(row_count, col_count, rows, width)
    return jnp.transpose(parts, (0, 2, 1, 3)).reshape(row_count * rows, col_count * width)


def join_columns(piece):
    row_count, col_count = lax.axis_size("row"), lax.axis_size("col")
    total, width = piece.shape
    rows = total // row_count
    parts = lax.all_to_all(
        piece.reshape(row_count, rows, width), "row", split_axis=0, concat_axis=0, tiled=True
    )
    parts = lax.all_gather(parts, "col", axis=0, tiled=False)
    parts = parts.reshape(col_count, row_count, rows, width // LANE, LANE)
    return jnp.transpose(parts, (2, 3, 1, 0, 4)).reshape(rows, -1)


def spread_poles(values, live, limit, masked):
    values = values[:limit]
    if masked:
        values = jnp.where(jnp.arange(limit, dtype=jnp.int32) < live, values, 0.0)
    return jnp.broadcast_to(values[:, None], (limit, LANE))


def shards(
    eigen_rows,
    live_one,
    order_one,
    poles_one,
    weights_one,
    roots_one,
    live_two,
    order_two,
    poles_two,
    weights_two,
    roots_two,
):
    col_count, row_count = lax.axis_size("col"), lax.axis_size("row")
    col_index, row_index = lax.axis_index("col"), lax.axis_index("row")
    merge_index = lax.axis_index("merge")
    merge_order = order_one.shape[1]
    group, member = row_count * col_count, row_index * col_count + col_index
    most = 3 * merge_order // 8
    pole_limit = ceil_to(most, max(POLE_TILE, LANE * col_count))
    share = pole_limit // col_count
    wide_one = ceil_to(most, LANE * group)
    wide_two = ceil_to(2 * most, LANE * group)
    out_width = 2 * merge_order // col_count
    zero = jnp.zeros((), jnp.int32)

    half = merge_index % 2
    pair_first = merge_index - half
    count_first, count_second = live_two[pair_first], live_two[pair_first + 1]
    count_own = live_two[merge_index]
    joined = count_first + count_second
    pairs = [(k, k ^ 1) for k in range(lax.axis_size("merge"))]
    own_roots = roots_two[0, :most]
    other_roots = lax.ppermute(own_roots, "merge", pairs)
    roots_first = jnp.where(half == 0, own_roots, other_roots)
    roots_second = jnp.where(half == 0, other_roots, own_roots)
    columns = jnp.arange(wide_two, dtype=jnp.int32)
    from_first = columns < count_first
    padded_first = jnp.concatenate([roots_first, jnp.zeros((wide_two - most,), jnp.float32)])
    padded_second = jnp.concatenate(
        [jnp.zeros((most,), jnp.float32), roots_second, jnp.zeros((wide_two,), jnp.float32)]
    )
    moved_second = lax.dynamic_slice_in_dim(padded_second, most - count_first, wide_two)
    root_shift = jnp.where(from_first, padded_first, moved_second)
    root_shift = jnp.where(columns < joined, root_shift, 0.5)
    root_place = jnp.where(from_first, 2 * columns, 2 * (columns - count_first) + 1)
    root_place = own_blocks(root_place.astype(jnp.float32), group, member)
    root_shift = own_blocks(root_shift, group, member)
    blocks_two = block_share(joined, group, member)
    info_two = jnp.stack([count_own, half, blocks_two]).astype(jnp.int32)
    shift_two = spread_poles(poles_two[0], count_own, pole_limit, False)
    weight_two = spread_poles(weights_two[0], count_own, pole_limit, True)
    sums_two = column_norms(2, info_two, shift_two, weight_two, root_place, root_shift)
    sums_two = sums_two + lax.ppermute(sums_two, "merge", pairs)

    live = live_one[merge_index]
    first = col_index * share
    gathered = lax.all_gather(eigen_rows[0], "col", axis=1, tiled=True)
    picked = pick_one(jnp.stack([first, live]).astype(jnp.int32), order_one[0], gathered, share)
    rows_one = join_rows(picked)
    column_one = jnp.arange(wide_one, dtype=jnp.int32).astype(jnp.float32)
    place_one = own_blocks(column_one, group, member)
    root_one = own_blocks(roots_one[0, :wide_one], group, member)
    info_one = jnp.stack([live, zero, block_share(live, group, member)]).astype(jnp.int32)
    shift_one = spread_poles(poles_one[0], live, pole_limit, False)
    weight_one = spread_poles(weights_one[0], live, pole_limit, True)
    sums_one = column_norms(1, info_one, shift_one, weight_one, place_one, root_one)
    level = cauchy_product(
        1, info_one, rows_one, shift_one, weight_one, place_one, root_one, 1.0 / jnp.sqrt(sums_one)
    )
    level = join_columns(level)

    slots = jnp.arange(merge_order, dtype=jnp.int32)
    place = jnp.where(slots < live, slots, wide_one + order_one[0])
    begin = col_index * out_width
    offset = jnp.where(half == 0, -count_second, -merge_order)
    low = jnp.where(half == 0, joined, merge_order + count_second)
    high = jnp.where(half == 0, merge_order + count_second, 2 * merge_order)
    low = jnp.clip(low - begin, 0, out_width)
    high = jnp.clip(high - begin, 0, out_width)
    info_pick = jnp.stack([first, count_own, offset + begin, low, high]).astype(jnp.int32)
    picked, moved = pick_two(
        info_pick, order_two[0], place, level, gathered, share, out_width
    )
    rows_two = join_rows(picked)
    mixed = cauchy_product(
        2,
        info_two,
        rows_two,
        shift_two,
        weight_two,
        root_place,
        root_shift,
        1.0 / jnp.sqrt(sums_two),
    )
    mixed = join_columns(mixed)
    mixed = jnp.pad(mixed, ((0, 0), (0, 2 * merge_order - wide_two)))
    mixed = lax.dynamic_slice_in_dim(mixed, begin, out_width, 1)
    local = jnp.arange(out_width, dtype=jnp.int32)
    keep = (local >= low) & (local < high)
    moved = jnp.where(keep[None, :], moved, jnp.zeros((), jnp.bfloat16))
    result = jnp.where((local + begin < joined)[None, :], mixed, moved)
    return result[None]


def solution(mesh):
    placed = (
        P("merge", "row", "col"),
        P(),
        P("merge", None),
        P("merge", None),
        P("merge", None),
        P("merge", None),
        P(),
        P("merge", None),
        P("merge", None),
        P("merge", None),
        P("merge", None),
    )
    return jax.shard_map(
        shards, mesh=mesh, in_specs=placed, out_specs=P("merge", "row", "col"), check_vma=False
    )
```

```python
import functools

import jax
import jax.numpy as jnp
from jax import lax
from jax.experimental import pallas as pl
from jax.experimental.pallas import tpu as pltpu
from jax.sharding import PartitionSpec as P

LANE = 128
POLE_TILE = 512
VMEM_LIMIT = 56 * 1024 * 1024


def inverse_of(distance):
    guess = pl.reciprocal(distance, approx=True)
    return guess * (2.0 - distance * guess)


def spec(space):
    return pl.BlockSpec(memory_space=space)


def fill_table(source_ref, table_ref):
    rows, width = source_ref.shape
    blocks = width // LANE
    unroll = 8 if blocks % 8 == 0 else 1

    def some(turn, carry):
        for k in range(unroll):
            opening = pl.multiple_of((turn * unroll + k) * LANE, LANE)
            block = source_ref[:, pl.ds(opening, LANE)].astype(jnp.float32)
            table_ref[pl.ds(opening, LANE), 0:rows] = block.T
        return carry

    lax.fori_loop(0, blocks // unroll, some, 0)


def pick_block(table_ref, stage_ref, index_of, rows):
    for k in range(LANE):
        stage_ref[k : k + 1, :] = table_ref[pl.ds(index_of(k), 1), :]
    return stage_ref[...].T[0:rows, :].astype(jnp.bfloat16)


def pick_one_kernel(info_ref, order_ref, source_ref, out_ref, table_ref, stage_ref):
    rows = source_ref.shape[0]
    table_ref[...] = jnp.zeros(table_ref.shape, jnp.float32)
    fill_table(source_ref, table_ref)
    out_ref[...] = jnp.zeros(out_ref.shape, out_ref.dtype)
    first, live = info_ref[0], info_ref[1]
    count = jnp.clip((live - first + LANE - 1) // LANE, 0, out_ref.shape[1] // LANE)

    def one(step, carry):
        opening = pl.multiple_of(step * LANE, LANE)
        out_ref[:, pl.ds(opening, LANE)] = pick_block(
            table_ref, stage_ref, lambda k: order_ref[first + opening + k], rows
        )
        return carry

    lax.fori_loop(0, count, one, 0)


def pick_one(info, order, source, width):
    rows, total = source.shape
    return pl.pallas_call(
        pick_one_kernel,
        out_shape=(
            jax.ShapeDtypeStruct((rows, width), jnp.bfloat16),
            jax.ShapeDtypeStruct((total, LANE), jnp.float32),
        ),
        in_specs=[spec(pltpu.SMEM), spec(pltpu.SMEM), spec(pltpu.VMEM)],
        out_specs=(spec(pltpu.VMEM), spec(pltpu.VMEM)),
        scratch_shapes=[pltpu.VMEM((LANE, LANE), jnp.float32)],
        compiler_params=pltpu.CompilerParams(vmem_limit_bytes=VMEM_LIMIT),
    )(info, order, source)


def pick_two_kernel(
    stride,
    info_ref,
    order_ref,
    place_ref,
    level_ref,
    source_ref,
    out_ref,
    moved_ref,
    table_ref,
    stage_ref,
    copy_sem,
):
    rows, wide = level_ref.shape
    copy = pltpu.make_async_copy(
        source_ref, table_ref.at[pl.ds(wide, source_ref.shape[0])], copy_sem
    )
    copy.start()
    out_ref[...] = jnp.zeros(out_ref.shape, out_ref.dtype)
    moved_ref[...] = jnp.zeros(moved_ref.shape, moved_ref.dtype)
    table_ref[0:wide, :] = jnp.zeros((wide, LANE), jnp.float32)
    fill_table(level_ref, table_ref)
    copy.wait()
    first, live = info_ref[0], info_ref[1]
    count = jnp.clip((live - first + LANE - 1) // LANE, 0, out_ref.shape[1] // LANE)

    def one(step, carry):
        opening = pl.multiple_of(step * LANE, LANE)
        out_ref[:, pl.ds(opening, LANE)] = pick_block(
            table_ref, stage_ref, lambda k: place_ref[order_ref[first + opening + k]], rows
        )
        return carry

    lax.fori_loop(0, count, one, 0)
    offset, low, high = info_ref[2], info_ref[3], info_ref[4]

    def other(step, carry):
        opening = pl.multiple_of(step * LANE, LANE)
        begin = offset + step * stride
        moved_ref[:, pl.ds(opening, LANE)] = pick_block(
            table_ref, stage_ref, lambda k: place_ref[order_ref[begin + k]], rows
        )
        return carry

    lax.fori_loop(low, high, other, 0)


def pick_two(stride, info, order, place, level, table, width, moved_width):
    rows, wide = level.shape
    return pl.pallas_call(
        functools.partial(pick_two_kernel, stride),
        out_shape=(
            jax.ShapeDtypeStruct((rows, width), jnp.bfloat16),
            jax.ShapeDtypeStruct((rows, moved_width), jnp.bfloat16),
        ),
        in_specs=[spec(pltpu.SMEM)] * 3 + [spec(pltpu.VMEM), spec(pl.ANY)],
        out_specs=(spec(pltpu.VMEM), spec(pltpu.VMEM)),
        scratch_shapes=[
            pltpu.VMEM((table.shape[0] + wide, LANE), jnp.float32),
            pltpu.VMEM((LANE, LANE), jnp.float32),
            pltpu.SemaphoreType.DMA,
        ],
        compiler_params=pltpu.CompilerParams(vmem_limit_bytes=VMEM_LIMIT),
    )(info, order, place, level, table)


def wide_columns(values):
    width = 2 * LANE if values.shape[0] % 2 == 0 else LANE
    return values.reshape(-1, width)


def across(values, width):
    return jnp.concatenate([values] * (width // LANE), axis=1)


def quotients(start, rows, stride, half, shift_ref, weight_ref, place, root):
    width = place.shape[1]
    slot = lax.broadcasted_iota(jnp.int32, (rows, LANE), 0) + start
    poles = across((slot * stride + half).astype(jnp.float32), width)
    shifts = across(shift_ref[pl.ds(start, rows), :], width)
    distance = (poles - place) + (shifts - root)
    return across(weight_ref[pl.ds(start, rows), :], width) * inverse_of(distance)


def norm_kernel(stride, info_ref, shift_ref, weight_ref, place_ref, root_ref, out_ref):
    live, half, blocks = info_ref[0], info_ref[1], info_ref[2]
    tiles = (live + POLE_TILE - 1) // POLE_TILE
    width = place_ref.shape[1]
    turns = (blocks * LANE + width - 1) // width
    out_ref[...] = jnp.ones(out_ref.shape, jnp.float32)

    def one_block(block, carry):
        place = place_ref[pl.ds(block, 1), :]
        root = root_ref[pl.ds(block, 1), :]

        def one_tile(tile, running):
            opening = pl.multiple_of(tile * POLE_TILE, POLE_TILE)
            for part in range(POLE_TILE // 32):
                term = quotients(
                    opening + part * 32, 32, stride, half, shift_ref, weight_ref, place, root
                )
                running = running + jnp.sum((term * term).reshape(4, 8, width), axis=0)
            return running

        sums = lax.fori_loop(0, tiles, one_tile, jnp.zeros((8, width), jnp.float32))
        out_ref[pl.ds(block, 1), :] = jnp.sum(sums, axis=0, keepdims=True)
        return carry

    lax.fori_loop(0, turns, one_block, 0)


def column_norms(stride, info, shift, weight, place, root):
    work = shift.shape[0] * place.size
    return pl.pallas_call(
        functools.partial(norm_kernel, stride),
        out_shape=jax.ShapeDtypeStruct(place.shape, jnp.float32),
        in_specs=[spec(pltpu.SMEM)] + [spec(pltpu.VMEM)] * 4,
        out_specs=spec(pltpu.VMEM),
        cost_estimate=pl.CostEstimate(
            flops=3000 * work, bytes_accessed=8 * work, transcendentals=work
        ),
        compiler_params=pltpu.CompilerParams(vmem_limit_bytes=VMEM_LIMIT),
    )(info, shift, weight, place, root)


def apply_kernel(
    stride, info_ref, rows_ref, shift_ref, weight_ref, place_ref, root_ref, inverse_ref, out_ref
):
    live, half, blocks = info_ref[0], info_ref[1], info_ref[2]
    tiles = (live + POLE_TILE - 1) // POLE_TILE
    row_total = rows_ref.shape[0]
    width = place_ref.shape[1]
    turns = (blocks * LANE + width - 1) // width
    out_ref[...] = jnp.zeros(out_ref.shape, out_ref.dtype)

    def one_block(block, carry):
        place = place_ref[pl.ds(block, 1), :]
        root = root_ref[pl.ds(block, 1), :]
        inverse = inverse_ref[pl.ds(block, 1), :]

        def one_tile(tile, running):
            opening = pl.multiple_of(tile * POLE_TILE, POLE_TILE)
            pieces = []
            for part in range(POLE_TILE // 32):
                term = quotients(
                    opening + part * 32, 32, stride, half, shift_ref, weight_ref, place, root
                )
                pieces.append((term * inverse).astype(jnp.bfloat16))
            return running + jnp.dot(
                rows_ref[:, pl.ds(opening, POLE_TILE)],
                jnp.concatenate(pieces, axis=0),
                preferred_element_type=jnp.float32,
            )

        total = lax.fori_loop(0, tiles, one_tile, jnp.zeros((row_total, width), jnp.float32))
        out_ref[:, pl.ds(pl.multiple_of(block * width, width), width)] = total.astype(
            out_ref.dtype
        )
        return carry

    lax.fori_loop(0, turns, one_block, 0)


def cauchy_product(stride, info, rows, shift, weight, place, root, inverse):
    return pl.pallas_call(
        functools.partial(apply_kernel, stride),
        out_shape=jax.ShapeDtypeStruct((rows.shape[0], place.size), jnp.bfloat16),
        in_specs=[spec(pltpu.SMEM)] + [spec(pltpu.VMEM)] * 6,
        out_specs=spec(pltpu.VMEM),
        compiler_params=pltpu.CompilerParams(vmem_limit_bytes=VMEM_LIMIT),
    )(info, rows, shift, weight, place, root, inverse)


def ceil_to(value, unit):
    return (value + unit - 1) // unit * unit


def own_blocks(values, group, member):
    spread = values.reshape(-1, group, LANE)
    return lax.dynamic_index_in_dim(spread, member, 1, keepdims=False)


def block_share(live, group, member):
    total = (live + LANE - 1) // LANE
    return jnp.maximum((total - member + group - 1) // group, 0)


def join_rows(piece):
    rows, width = piece.shape
    row_count, col_count = lax.axis_size("row"), lax.axis_size("col")
    parts = lax.all_gather(piece, ("row", "col"), axis=0, tiled=False)
    parts = parts.reshape(row_count, col_count, rows, width)
    return jnp.transpose(parts, (0, 2, 1, 3)).reshape(row_count * rows, col_count * width)


def join_blocks(piece):
    row_count = lax.axis_size("row")
    total, width = piece.shape
    rows = total // row_count
    parts = lax.all_to_all(
        piece.reshape(row_count, rows, width), "row", split_axis=0, concat_axis=0, tiled=True
    )
    parts = parts.reshape(row_count, rows, width // LANE, LANE)
    return jnp.transpose(parts, (1, 2, 0, 3)).reshape(rows, -1)


def join_columns(piece):
    parts = join_blocks(piece)
    rows, width = parts.shape
    parts = lax.all_gather(parts, "col", axis=0, tiled=False)
    parts = parts.reshape(lax.axis_size("col"), rows, width // LANE, LANE)
    return jnp.transpose(parts, (1, 2, 0, 3)).reshape(rows, -1)


def spread_poles(values, live, limit, masked):
    values = values[:limit]
    if masked:
        values = jnp.where(jnp.arange(limit, dtype=jnp.int32) < live, values, 0.0)
    return jnp.broadcast_to(values[:, None], (limit, LANE))


def shards(
    eigen_rows,
    live_one,
    order_one,
    poles_one,
    weights_one,
    roots_one,
    live_two,
    order_two,
    poles_two,
    weights_two,
    roots_two,
):
    col_count, row_count = lax.axis_size("col"), lax.axis_size("row")
    col_index, row_index = lax.axis_index("col"), lax.axis_index("row")
    merge_index = lax.axis_index("merge")
    merge_order = order_one.shape[1]
    group, member = row_count * col_count, row_index * col_count + col_index
    most = 3 * merge_order // 8
    pole_limit = ceil_to(most, max(POLE_TILE, LANE * col_count))
    share = pole_limit // col_count
    wide_one = ceil_to(most, LANE * group)
    wide_two = ceil_to(2 * most, LANE * group)
    out_width = 2 * merge_order // col_count
    zero = jnp.zeros((), jnp.int32)

    half = merge_index % 2
    pair_first = merge_index - half
    count_first, count_second = live_two[pair_first], live_two[pair_first + 1]
    count_own = live_two[merge_index]
    joined = count_first + count_second
    pairs = [(k, k ^ 1) for k in range(lax.axis_size("merge"))]
    own_roots = roots_two[0, :most]
    other_roots = lax.ppermute(own_roots, "merge", pairs)
    roots_first = jnp.where(half == 0, own_roots, other_roots)
    roots_second = jnp.where(half == 0, other_roots, own_roots)
    columns = jnp.arange(wide_two, dtype=jnp.int32)
    from_first = columns < count_first
    padded_first = jnp.concatenate([roots_first, jnp.zeros((wide_two - most,), jnp.float32)])
    padded_second = jnp.concatenate(
        [jnp.zeros((most,), jnp.float32), roots_second, jnp.zeros((wide_two,), jnp.float32)]
    )
    moved_second = lax.dynamic_slice_in_dim(padded_second, most - count_first, wide_two)
    root_shift = jnp.where(from_first, padded_first, moved_second)
    root_shift = jnp.where(columns < joined, root_shift, 0.5)
    root_place = jnp.where(from_first, 2 * columns, 2 * (columns - count_first) + 1)
    root_place = wide_columns(own_blocks(root_place.astype(jnp.float32), group, member))
    root_shift = wide_columns(own_blocks(root_shift, group, member))
    blocks_two = block_share(joined, group, member)
    info_two = jnp.stack([count_own, half, blocks_two]).astype(jnp.int32)
    shift_two = spread_poles(poles_two[0], count_own, pole_limit, False)
    weight_two = spread_poles(weights_two[0], count_own, pole_limit, True)
    sums_two = column_norms(2, info_two, shift_two, weight_two, root_place, root_shift)
    sums_two = sums_two + lax.ppermute(sums_two, "merge", pairs)

    live = live_one[merge_index]
    first = col_index * share
    gathered = lax.all_gather(eigen_rows[0], "col", axis=1, tiled=True)
    picked, table = pick_one(jnp.stack([first, live]).astype(jnp.int32), order_one[0], gathered, share)
    rows_one = join_rows(picked)
    column_one = jnp.arange(wide_one, dtype=jnp.int32).astype(jnp.float32)
    place_one = wide_columns(own_blocks(column_one, group, member))
    root_one = wide_columns(own_blocks(roots_one[0, :wide_one], group, member))
    info_one = jnp.stack([live, zero, block_share(live, group, member)]).astype(jnp.int32)
    shift_one = spread_poles(poles_one[0], live, pole_limit, False)
    weight_one = spread_poles(weights_one[0], live, pole_limit, True)
    sums_one = column_norms(1, info_one, shift_one, weight_one, place_one, root_one)
    level = cauchy_product(
        1, info_one, rows_one, shift_one, weight_one, place_one, root_one, 1.0 / jnp.sqrt(sums_one)
    )
    level = join_columns(level)

    slots = jnp.arange(merge_order, dtype=jnp.int32)
    place = jnp.where(slots < live, slots, wide_one + order_one[0])
    offset = jnp.where(half == 0, -count_second, -merge_order)
    low = jnp.where(half == 0, joined, merge_order + count_second)
    high = jnp.where(half == 0, merge_order + count_second, 2 * merge_order)
    low_block, high_block = low // LANE, (high + LANE - 1) // LANE
    low_turn = (low_block - col_index + col_count - 1) // col_count
    high_turn = (high_block - col_index + col_count - 1) // col_count
    info_pick = jnp.stack(
        [first, count_own, offset + col_index * LANE, low_turn, high_turn]
    ).astype(jnp.int32)
    order_pad = jnp.pad(order_two[0], (0, LANE))
    picked, moved = pick_two(
        col_count * LANE, info_pick, order_pad, place, level, table, share, out_width
    )
    rows_two = join_rows(picked)
    mixed = cauchy_product(
        2,
        info_two,
        rows_two,
        shift_two,
        weight_two,
        root_place,
        root_shift,
        1.0 / jnp.sqrt(sums_two),
    )
    mixed = join_blocks(mixed)
    mixed = jnp.pad(mixed, ((0, 0), (0, out_width - mixed.shape[1])))
    local = jnp.arange(out_width, dtype=jnp.int32)
    own = (local // LANE * col_count + col_index) * LANE + local % LANE
    keep = (own >= low) & (own < high)
    moved = jnp.where(keep[None, :], moved, jnp.zeros((), jnp.bfloat16))
    result = jnp.where((own < joined)[None, :], mixed, moved)
    rows = result.shape[0]
    result = lax.all_to_all(
        result.reshape(rows, col_count, out_width // col_count),
        "col",
        split_axis=1,
        concat_axis=1,
        tiled=True,
    )
    result = result.reshape(rows, col_count, -1, LANE)
    return jnp.transpose(result, (0, 2, 1, 3)).reshape(1, rows, out_width)


def solution(mesh):
    placed = (
        P("merge", "row", "col"),
        P(),
        P("merge", None),
        P("merge", None),
        P("merge", None),
        P("merge", None),
        P(),
        P("merge", None),
        P("merge", None),
        P("merge", None),
        P("merge", None),
    )
    return jax.shard_map(
        shards, mesh=mesh, in_specs=placed, out_specs=P("merge", "row", "col"), check_vma=False
    )
```

```python
import functools

import jax
import jax.numpy as jnp
from jax import lax
from jax.experimental import pallas as pl
from jax.experimental.pallas import tpu as pltpu
from jax.sharding import PartitionSpec as P

LANE = 128
POLE_TILE = 512
VMEM_LIMIT = 56 * 1024 * 1024
MESH = pl.DeviceIdType.MESH


def inverse_of(distance):
    guess = pl.reciprocal(distance, approx=True)
    return guess * (2.0 - distance * guess)


def spec(space):
    return pl.BlockSpec(memory_space=space)


def fill_table(source_ref, table_ref, start=0):
    rows, width = source_ref.shape
    blocks = width // LANE
    unroll = max(k for k in (8, 6, 4, 3, 2, 1) if blocks % k == 0)

    def some(turn, carry):
        for k in range(unroll):
            opening = pl.multiple_of((turn * unroll + k) * LANE, LANE)
            block = source_ref[:, pl.ds(opening, LANE)].astype(jnp.float32)
            table_ref[pl.ds(start + opening, LANE), 0:rows] = block.T
        return carry

    lax.fori_loop(0, blocks // unroll, some, 0)


def pick_block(table_ref, stage_ref, index_of, rows):
    for k in range(LANE):
        stage_ref[k : k + 1, :] = table_ref[pl.ds(index_of(k), 1), :]
    return stage_ref[...].T[0:rows, :].astype(jnp.bfloat16)


def pick_one_kernel(info_ref, order_ref, source_ref, out_ref, table_ref, stage_ref):
    rows = source_ref.shape[0]
    table_ref[...] = jnp.zeros(table_ref.shape, jnp.float32)
    fill_table(source_ref, table_ref)
    out_ref[...] = jnp.zeros(out_ref.shape, out_ref.dtype)
    first, live = info_ref[0], info_ref[1]
    count = jnp.clip((live - first + LANE - 1) // LANE, 0, out_ref.shape[1] // LANE)

    def one(step, carry):
        opening = pl.multiple_of(step * LANE, LANE)
        out_ref[:, pl.ds(opening, LANE)] = pick_block(
            table_ref, stage_ref, lambda k: order_ref[first + opening + k], rows
        )
        return carry

    lax.fori_loop(0, count, one, 0)


def pick_one(info, order, source, width):
    rows, total = source.shape
    return pl.pallas_call(
        pick_one_kernel,
        out_shape=(
            jax.ShapeDtypeStruct((rows, width), jnp.bfloat16),
            jax.ShapeDtypeStruct((total, LANE), jnp.float32),
        ),
        in_specs=[spec(pltpu.SMEM), spec(pltpu.SMEM), spec(pltpu.VMEM)],
        out_specs=(spec(pltpu.VMEM), spec(pltpu.VMEM)),
        scratch_shapes=[pltpu.VMEM((LANE, LANE), jnp.float32)],
        compiler_params=pltpu.CompilerParams(vmem_limit_bytes=VMEM_LIMIT),
    )(info, order, source)


def pick_two_kernel(
    stride,
    info_ref,
    order_ref,
    place_ref,
    level_ref,
    source_ref,
    out_ref,
    moved_ref,
    table_ref,
    stage_ref,
    copy_sem,
):
    group, rows, width = level_ref.shape
    wide = group * width
    copy = pltpu.make_async_copy(
        source_ref, table_ref.at[pl.ds(wide, source_ref.shape[0])], copy_sem
    )
    copy.start()
    out_ref[...] = jnp.zeros(out_ref.shape, out_ref.dtype)
    moved_ref[...] = jnp.zeros(moved_ref.shape, moved_ref.dtype)
    table_ref[0:wide, :] = jnp.zeros((wide, LANE), jnp.float32)
    for part in range(group):
        fill_table(level_ref.at[part], table_ref, part * width)
    copy.wait()
    first, live = info_ref[0], info_ref[1]
    count = jnp.clip((live - first + LANE - 1) // LANE, 0, out_ref.shape[1] // LANE)

    def one(step, carry):
        opening = pl.multiple_of(step * LANE, LANE)
        out_ref[:, pl.ds(opening, LANE)] = pick_block(
            table_ref, stage_ref, lambda k: place_ref[order_ref[first + opening + k]], rows
        )
        return carry

    lax.fori_loop(0, count, one, 0)
    offset, low, high = info_ref[2], info_ref[3], info_ref[4]

    def other(step, carry):
        opening = pl.multiple_of(step * LANE, LANE)
        begin = offset + step * stride
        moved_ref[:, pl.ds(opening, LANE)] = pick_block(
            table_ref, stage_ref, lambda k: place_ref[order_ref[begin + k]], rows
        )
        return carry

    lax.fori_loop(low, high, other, 0)


def pick_two(stride, info, order, place, level, table, width, moved_width):
    group, rows, wide = level.shape
    wide = wide * group
    return pl.pallas_call(
        functools.partial(pick_two_kernel, stride),
        out_shape=(
            jax.ShapeDtypeStruct((rows, width), jnp.bfloat16),
            jax.ShapeDtypeStruct((rows, moved_width), jnp.bfloat16),
        ),
        in_specs=[spec(pltpu.SMEM)] * 3 + [spec(pltpu.VMEM), spec(pl.ANY)],
        out_specs=(spec(pltpu.VMEM), spec(pltpu.VMEM)),
        scratch_shapes=[
            pltpu.VMEM((table.shape[0] + wide, LANE), jnp.float32),
            pltpu.VMEM((LANE, LANE), jnp.float32),
            pltpu.SemaphoreType.DMA,
        ],
        compiler_params=pltpu.CompilerParams(vmem_limit_bytes=VMEM_LIMIT),
    )(info, order, place, level, table)


def wide_columns(values):
    width = 2 * LANE if values.shape[0] % 2 == 0 else LANE
    return values.reshape(-1, width)


def across(values, width):
    return jnp.concatenate([values] * (width // LANE), axis=1)


def quotients(start, rows, stride, half, shift_ref, weight_ref, place, root):
    width = place.shape[1]
    slot = lax.broadcasted_iota(jnp.int32, (rows, LANE), 0) + start
    poles = across((slot * stride + half).astype(jnp.float32), width)
    shifts = across(shift_ref[pl.ds(start, rows), :], width)
    distance = (poles - place) + (shifts - root)
    return across(weight_ref[pl.ds(start, rows), :], width) * inverse_of(distance)


def norm_kernel(stride, info_ref, shift_ref, weight_ref, place_ref, root_ref, out_ref):
    live, half, blocks = info_ref[0], info_ref[1], info_ref[2]
    tiles = (live + POLE_TILE - 1) // POLE_TILE
    width = place_ref.shape[1]
    turns = (blocks * LANE + width - 1) // width
    out_ref[...] = jnp.ones(out_ref.shape, jnp.float32)

    def one_block(block, carry):
        place = place_ref[pl.ds(block, 1), :]
        root = root_ref[pl.ds(block, 1), :]

        def one_tile(tile, running):
            opening = pl.multiple_of(tile * POLE_TILE, POLE_TILE)
            for part in range(POLE_TILE // 32):
                term = quotients(
                    opening + part * 32, 32, stride, half, shift_ref, weight_ref, place, root
                )
                running = running + jnp.sum((term * term).reshape(4, 8, width), axis=0)
            return running

        sums = lax.fori_loop(0, tiles, one_tile, jnp.zeros((8, width), jnp.float32))
        out_ref[pl.ds(block, 1), :] = jnp.sum(sums, axis=0, keepdims=True)
        return carry

    lax.fori_loop(0, turns, one_block, 0)


def column_norms(stride, info, shift, weight, place, root):
    work = shift.shape[0] * place.size
    return pl.pallas_call(
        functools.partial(norm_kernel, stride),
        out_shape=jax.ShapeDtypeStruct(place.shape, jnp.float32),
        in_specs=[spec(pltpu.SMEM)] + [spec(pltpu.VMEM)] * 4,
        out_specs=spec(pltpu.VMEM),
        cost_estimate=pl.CostEstimate(
            flops=3000 * work, bytes_accessed=8 * work, transcendentals=work
        ),
        compiler_params=pltpu.CompilerParams(vmem_limit_bytes=VMEM_LIMIT),
    )(info, shift, weight, place, root)


def apply_kernel(
    stride, info_ref, rows_ref, shift_ref, weight_ref, place_ref, root_ref, inverse_ref, out_ref
):
    live, half, blocks = info_ref[0], info_ref[1], info_ref[2]
    tiles = (live + POLE_TILE - 1) // POLE_TILE
    row_total = rows_ref.shape[0]
    width = place_ref.shape[1]
    turns = (blocks * LANE + width - 1) // width
    out_ref[...] = jnp.zeros(out_ref.shape, out_ref.dtype)

    def one_block(block, carry):
        place = place_ref[pl.ds(block, 1), :]
        root = root_ref[pl.ds(block, 1), :]
        inverse = inverse_ref[pl.ds(block, 1), :]

        def one_tile(tile, running):
            opening = pl.multiple_of(tile * POLE_TILE, POLE_TILE)
            pieces = []
            for part in range(POLE_TILE // 32):
                term = quotients(
                    opening + part * 32, 32, stride, half, shift_ref, weight_ref, place, root
                )
                pieces.append((term * inverse).astype(jnp.bfloat16))
            return running + jnp.dot(
                rows_ref[:, pl.ds(opening, POLE_TILE)],
                jnp.concatenate(pieces, axis=0),
                preferred_element_type=jnp.float32,
            )

        total = lax.fori_loop(0, tiles, one_tile, jnp.zeros((row_total, width), jnp.float32))
        out_ref[:, pl.ds(pl.multiple_of(block * width, width), width)] = total.astype(
            out_ref.dtype
        )
        return carry

    lax.fori_loop(0, turns, one_block, 0)


def cauchy_product(stride, info, rows, shift, weight, place, root, inverse):
    return pl.pallas_call(
        functools.partial(apply_kernel, stride),
        out_shape=jax.ShapeDtypeStruct((rows.shape[0], place.size), jnp.bfloat16),
        in_specs=[spec(pltpu.SMEM)] + [spec(pltpu.VMEM)] * 6,
        out_specs=spec(pltpu.VMEM),
        cost_estimate=pl.CostEstimate(
            flops=3000 * shift.shape[0] * place.size, bytes_accessed=0, transcendentals=0
        ),
        compiler_params=pltpu.CompilerParams(vmem_limit_bytes=VMEM_LIMIT),
    )(info, rows, shift, weight, place, root, inverse)


def ceil_to(value, unit):
    return (value + unit - 1) // unit * unit


def own_blocks(values, group, member):
    spread = values.reshape(-1, group, LANE)
    return lax.dynamic_index_in_dim(spread, member, 1, keepdims=False)


def block_share(live, group, member):
    total = (live + LANE - 1) // LANE
    return jnp.maximum((total - member + group - 1) // group, 0)


def exchange_kernel(
    row_count, col_count, in_place, source_ref, out_ref, send_sem, recv_sem, own_sem
):
    merge = lax.axis_index("merge")
    row, col = lax.axis_index("row"), lax.axis_index("col")
    group = row_count * col_count
    me = row * col_count + col
    others = []
    for k in range(1, group):
        peer = lax.rem(me + k, group)
        others.append((merge, peer // col_count, lax.rem(peer, col_count)))
    barrier = pltpu.get_barrier_semaphore()
    for device in others:
        pl.semaphore_signal(barrier, inc=1, device_id=device, device_id_type=MESH)
    pl.semaphore_wait(barrier, group - 1)
    if in_place:
        rows, width = source_ref.shape
        target = out_ref.at[
            pl.ds(pl.multiple_of(row * rows, rows), rows),
            pl.ds(pl.multiple_of(col * width, width), width),
        ]
    else:
        target = out_ref.at[me]
    copies = []
    for k, device in enumerate(others):
        copy = pltpu.make_async_remote_copy(
            src_ref=source_ref if in_place else source_ref.at[device[1]],
            dst_ref=target,
            send_sem=send_sem.at[k],
            recv_sem=recv_sem.at[k],
            device_id=device,
            device_id_type=MESH,
        )
        copy.start()
        copies.append(copy)
    own = pltpu.make_async_copy(source_ref if in_place else source_ref.at[row], target, own_sem)
    own.start()
    own.wait()
    for copy in copies:
        copy.wait()


def exchange(source, in_place, number):
    row_count, col_count = lax.axis_size("row"), lax.axis_size("col")
    group = row_count * col_count
    rows, width = source.shape[-2:]
    shape = (row_count * rows, col_count * width) if in_place else (group, rows, width)
    return pl.pallas_call(
        functools.partial(exchange_kernel, row_count, col_count, in_place),
        out_shape=jax.ShapeDtypeStruct(shape, source.dtype),
        in_specs=[spec(pl.ANY)],
        out_specs=spec(pl.ANY),
        scratch_shapes=[
            pltpu.SemaphoreType.DMA((group - 1,)),
            pltpu.SemaphoreType.DMA((group - 1,)),
            pltpu.SemaphoreType.DMA,
        ],
        compiler_params=pltpu.CompilerParams(collective_id=number, has_side_effects=True),
    )(source)


def join_columns(piece, number):
    row_count = lax.axis_size("row")
    return exchange(piece.reshape(row_count, -1, piece.shape[1]), False, number)


def spread_moved(moved):
    col_count, col_index = lax.axis_size("col"), lax.axis_index("col")
    rows, width = moved.shape
    parts = moved.reshape(rows, col_count, width // col_count)
    pieces = jnp.zeros((col_count, rows, width // col_count), moved.dtype)
    for k in range(col_count):
        part = lax.dynamic_index_in_dim(parts, (col_index + k) % col_count, 1, keepdims=False)
        if k:
            pairs = [(c, (c + k) % col_count) for c in range(col_count)]
            part = lax.ppermute(part, "col", pairs)
        pieces = lax.dynamic_update_index_in_dim(
            pieces, part, (col_index - k + col_count) % col_count, 0
        )
    pieces = pieces.reshape(col_count, rows, -1, LANE)
    return jnp.transpose(pieces, (1, 2, 0, 3)).reshape(rows, width)


def spread_poles(values, live, limit, masked):
    values = values[:limit]
    if masked:
        values = jnp.where(jnp.arange(limit, dtype=jnp.int32) < live, values, 0.0)
    return jnp.broadcast_to(values[:, None], (limit, LANE))


def shards(
    eigen_rows,
    live_one,
    order_one,
    poles_one,
    weights_one,
    roots_one,
    live_two,
    order_two,
    poles_two,
    weights_two,
    roots_two,
):
    col_count, row_count = lax.axis_size("col"), lax.axis_size("row")
    col_index, row_index = lax.axis_index("col"), lax.axis_index("row")
    merge_index = lax.axis_index("merge")
    merge_order = order_one.shape[1]
    group, member = row_count * col_count, row_index * col_count + col_index
    most = 3 * merge_order // 8
    pole_limit = ceil_to(most, max(POLE_TILE, LANE * col_count))
    share = pole_limit // col_count
    wide_one = ceil_to(most, LANE * group)
    wide_two = ceil_to(2 * most, LANE * group)
    out_width = 2 * merge_order // col_count
    zero = jnp.zeros((), jnp.int32)

    half = merge_index % 2
    pair_first = merge_index - half
    count_first, count_second = live_two[pair_first], live_two[pair_first + 1]
    count_own = live_two[merge_index]
    joined = count_first + count_second
    pairs = [(k, k ^ 1) for k in range(lax.axis_size("merge"))]
    own_roots = roots_two[0, :most]
    other_roots = lax.ppermute(own_roots, "merge", pairs)
    roots_first = jnp.where(half == 0, own_roots, other_roots)
    roots_second = jnp.where(half == 0, other_roots, own_roots)
    columns = jnp.arange(wide_two, dtype=jnp.int32)
    from_first = columns < count_first
    padded_first = jnp.concatenate([roots_first, jnp.zeros((wide_two - most,), jnp.float32)])
    padded_second = jnp.concatenate(
        [jnp.zeros((most,), jnp.float32), roots_second, jnp.zeros((wide_two,), jnp.float32)]
    )
    moved_second = lax.dynamic_slice_in_dim(padded_second, most - count_first, wide_two)
    root_shift = jnp.where(from_first, padded_first, moved_second)
    root_shift = jnp.where(columns < joined, root_shift, 0.5)
    root_place = jnp.where(from_first, 2 * columns, 2 * (columns - count_first) + 1)
    root_place = wide_columns(own_blocks(root_place.astype(jnp.float32), group, member))
    root_shift = wide_columns(own_blocks(root_shift, group, member))
    blocks_two = block_share(joined, group, member)
    info_two = jnp.stack([count_own, half, blocks_two]).astype(jnp.int32)
    shift_two = spread_poles(poles_two[0], count_own, pole_limit, False)
    weight_two = spread_poles(weights_two[0], count_own, pole_limit, True)
    sums_two = column_norms(2, info_two, shift_two, weight_two, root_place, root_shift)
    sums_two = sums_two + lax.ppermute(sums_two, "merge", pairs)

    live = live_one[merge_index]
    first = col_index * share
    gathered = lax.all_gather(eigen_rows[0], "col", axis=1, tiled=True)
    column_one = jnp.arange(wide_one, dtype=jnp.int32).astype(jnp.float32)
    place_one = wide_columns(own_blocks(column_one, group, member))
    root_one = wide_columns(own_blocks(roots_one[0, :wide_one], group, member))
    info_one = jnp.stack([live, zero, block_share(live, group, member)]).astype(jnp.int32)
    shift_one = spread_poles(poles_one[0], live, pole_limit, False)
    weight_one = spread_poles(weights_one[0], live, pole_limit, True)
    sums_one = column_norms(1, info_one, shift_one, weight_one, place_one, root_one)
    inverse_one = 1.0 / jnp.sqrt(sums_one)
    inverse_two = 1.0 / jnp.sqrt(sums_two)
    gathered, inverse_one, inverse_two, weight_one, weight_two = lax.optimization_barrier(
        (gathered, inverse_one, inverse_two, weight_one, weight_two)
    )
    picked, table = pick_one(jnp.stack([first, live]).astype(jnp.int32), order_one[0], gathered, share)
    rows_one = exchange(picked, True, 0)
    level = cauchy_product(
        1, info_one, rows_one, shift_one, weight_one, place_one, root_one, inverse_one
    )
    level = join_columns(level, 1)

    slots = jnp.arange(merge_order, dtype=jnp.int32)
    slot_block = slots // LANE
    level_place = (slot_block % group * (wide_one // group // LANE) + slot_block // group) * LANE
    place = jnp.where(slots < live, level_place + slots % LANE, wide_one + order_one[0])
    offset = jnp.where(half == 0, -count_second, -merge_order)
    low = jnp.where(half == 0, joined, merge_order + count_second)
    high = jnp.where(half == 0, merge_order + count_second, 2 * merge_order)
    low_block, high_block = low // LANE, (high + LANE - 1) // LANE
    low_turn = (low_block - col_index + col_count - 1) // col_count
    high_turn = (high_block - col_index + col_count - 1) // col_count
    info_pick = jnp.stack(
        [first, count_own, offset + col_index * LANE, low_turn, high_turn]
    ).astype(jnp.int32)
    order_pad = jnp.pad(order_two[0], (0, LANE))
    picked, moved = pick_two(
        col_count * LANE, info_pick, order_pad, place, level, table, share, out_width
    )
    rows_two = exchange(picked, True, 2)
    mixed = cauchy_product(
        2,
        info_two,
        rows_two,
        shift_two,
        weight_two,
        root_place,
        root_shift,
        inverse_two,
    )
    mixed = join_columns(mixed, 3)
    rows = mixed.shape[1]
    mixed = mixed.reshape(group, rows, -1, LANE)
    mixed = jnp.transpose(mixed, (1, 2, 0, 3)).reshape(rows, wide_two)
    mixed = jnp.pad(mixed, ((0, 0), (0, 2 * merge_order - wide_two)))
    begin = col_index * out_width
    mixed = lax.dynamic_slice_in_dim(mixed, begin, out_width, 1)
    own = jnp.arange(out_width, dtype=jnp.int32) + begin
    keep = (own >= low) & (own < high)
    moved = jnp.where(keep[None, :], spread_moved(moved), jnp.zeros((), jnp.bfloat16))
    result = jnp.where((own < joined)[None, :], mixed, moved)
    return result[None]


def solution(mesh):
    placed = (
        P("merge", "row", "col"),
        P(),
        P("merge", None),
        P("merge", None),
        P("merge", None),
        P("merge", None),
        P(),
        P("merge", None),
        P("merge", None),
        P("merge", None),
        P("merge", None),
    )
    return jax.shard_map(
        shards, mesh=mesh, in_specs=placed, out_specs=P("merge", "row", "col"), check_vma=False
    )
```

```python
import functools

import jax
import jax.numpy as jnp
from jax import lax
from jax.experimental import pallas as pl
from jax.experimental.pallas import tpu as pltpu
from jax.sharding import PartitionSpec as P

LANE = 128
PART = 32
POLE_TILE = 1024
VMEM_LIMIT = 56 * 1024 * 1024
MESH = pl.DeviceIdType.MESH


def inverse_of(distance):
    guess = pl.reciprocal(distance, approx=True)
    return guess * (2.0 - distance * guess)


def spec(space):
    return pl.BlockSpec(memory_space=space)


def fill_table(source_ref, table_ref, start=0):
    rows, width = source_ref.shape
    blocks = width // LANE
    unroll = max(k for k in (8, 6, 4, 3, 2, 1) if blocks % k == 0)

    def some(turn, carry):
        for k in range(unroll):
            opening = pl.multiple_of((turn * unroll + k) * LANE, LANE)
            block = source_ref[:, pl.ds(opening, LANE)].astype(jnp.float32)
            table_ref[pl.ds(start + opening, LANE), 0:rows] = block.T
        return carry

    lax.fori_loop(0, blocks // unroll, some, 0)


def pick_block(table_ref, stage_ref, index_of, rows):
    for k in range(LANE):
        stage_ref[k : k + 1, :] = table_ref[pl.ds(index_of(k), 1), :]
    return stage_ref[...].T[0:rows, :].astype(jnp.bfloat16)


def pick_one_kernel(info_ref, order_ref, source_ref, out_ref, table_ref, stage_ref):
    rows = source_ref.shape[0]
    table_ref[...] = jnp.zeros(table_ref.shape, jnp.float32)
    fill_table(source_ref, table_ref)
    out_ref[...] = jnp.zeros(out_ref.shape, out_ref.dtype)
    first, live = info_ref[0], info_ref[1]
    count = jnp.clip((live - first + LANE - 1) // LANE, 0, out_ref.shape[1] // LANE)

    def one(step, carry):
        opening = pl.multiple_of(step * LANE, LANE)
        out_ref[:, pl.ds(opening, LANE)] = pick_block(
            table_ref, stage_ref, lambda k: order_ref[first + opening + k], rows
        )
        return carry

    lax.fori_loop(0, count, one, 0)


def pick_one(info, order, source, width):
    rows, total = source.shape
    return pl.pallas_call(
        pick_one_kernel,
        out_shape=(
            jax.ShapeDtypeStruct((rows, width), jnp.bfloat16),
            jax.ShapeDtypeStruct((total, LANE), jnp.float32),
        ),
        in_specs=[spec(pltpu.SMEM), spec(pltpu.SMEM), spec(pltpu.VMEM)],
        out_specs=(spec(pltpu.VMEM), spec(pltpu.VMEM)),
        scratch_shapes=[pltpu.VMEM((LANE, LANE), jnp.float32)],
        compiler_params=pltpu.CompilerParams(vmem_limit_bytes=VMEM_LIMIT),
    )(info, order, source)


def pick_two_kernel(
    stride,
    info_ref,
    order_ref,
    place_ref,
    level_ref,
    source_ref,
    out_ref,
    moved_ref,
    table_ref,
    stage_ref,
    copy_sem,
):
    group, rows, width = level_ref.shape
    wide = group * width
    copy = pltpu.make_async_copy(
        source_ref, table_ref.at[pl.ds(wide, source_ref.shape[0])], copy_sem
    )
    copy.start()
    out_ref[...] = jnp.zeros(out_ref.shape, out_ref.dtype)
    moved_ref[...] = jnp.zeros(moved_ref.shape, moved_ref.dtype)
    table_ref[0:wide, :] = jnp.zeros((wide, LANE), jnp.float32)
    for part in range(group):
        fill_table(level_ref.at[part], table_ref, part * width)
    copy.wait()
    first, live = info_ref[0], info_ref[1]
    count = jnp.clip((live - first + LANE - 1) // LANE, 0, out_ref.shape[1] // LANE)

    def one(step, carry):
        opening = pl.multiple_of(step * LANE, LANE)
        out_ref[:, pl.ds(opening, LANE)] = pick_block(
            table_ref, stage_ref, lambda k: place_ref[order_ref[first + opening + k]], rows
        )
        return carry

    lax.fori_loop(0, count, one, 0)
    offset, low, high = info_ref[2], info_ref[3], info_ref[4]

    per_part = moved_ref.shape[2] // LANE

    def other(step, carry):
        opening = pl.multiple_of(lax.rem(step, per_part) * LANE, LANE)
        begin = offset + step * stride
        moved_ref[step // per_part, :, pl.ds(opening, LANE)] = pick_block(
            table_ref, stage_ref, lambda k: place_ref[order_ref[begin + k]], rows
        )
        return carry

    lax.fori_loop(low, high, other, 0)


def pick_two(stride, info, order, place, level, table, width, moved_shape):
    group, rows, wide = level.shape
    wide = wide * group
    return pl.pallas_call(
        functools.partial(pick_two_kernel, stride),
        out_shape=(
            jax.ShapeDtypeStruct((rows, width), jnp.bfloat16),
            jax.ShapeDtypeStruct(moved_shape, jnp.bfloat16),
        ),
        in_specs=[spec(pltpu.SMEM)] * 3 + [spec(pltpu.VMEM), spec(pl.ANY)],
        out_specs=(spec(pltpu.VMEM), spec(pltpu.VMEM)),
        scratch_shapes=[
            pltpu.VMEM((table.shape[0] + wide, LANE), jnp.float32),
            pltpu.VMEM((LANE, LANE), jnp.float32),
            pltpu.SemaphoreType.DMA,
        ],
        compiler_params=pltpu.CompilerParams(vmem_limit_bytes=VMEM_LIMIT),
    )(info, order, place, level, table)


def wide_columns(values):
    width = 2 * LANE if values.shape[0] % 2 == 0 else LANE
    return values.reshape(-1, width)


def across(values, width):
    return jnp.concatenate([values] * (width // LANE), axis=1)


def offsets_from(place, stride, half):
    steps = lax.broadcasted_iota(jnp.int32, (PART, place.shape[1]), 0) * stride + half
    return steps.astype(jnp.float32) - place


def quotients(start, stride, offsets, shift_ref, weight_ref, root):
    width = root.shape[1]
    shifts = across(shift_ref[pl.ds(start, PART), :], width)
    distance = (offsets + (start * stride).astype(jnp.float32)) + (shifts - root)
    return across(weight_ref[pl.ds(start, PART), :], width) * inverse_of(distance)


def norm_kernel(stride, info_ref, shift_ref, weight_ref, place_ref, root_ref, out_ref):
    live, half, blocks = info_ref[0], info_ref[1], info_ref[2]
    tiles = (live + POLE_TILE - 1) // POLE_TILE
    width = place_ref.shape[1]
    turns = (blocks * LANE + width - 1) // width
    out_ref[...] = jnp.ones(out_ref.shape, jnp.float32)

    def one_block(block, carry):
        offsets = offsets_from(place_ref[pl.ds(block, 1), :], stride, half)
        root = root_ref[pl.ds(block, 1), :]

        def one_tile(tile, running):
            opening = pl.multiple_of(tile * POLE_TILE, POLE_TILE)
            for part in range(POLE_TILE // PART):
                term = quotients(
                    opening + part * PART, stride, offsets, shift_ref, weight_ref, root
                )
                running = running + jnp.sum((term * term).reshape(PART // 8, 8, width), axis=0)
            return running

        sums = lax.fori_loop(0, tiles, one_tile, jnp.zeros((8, width), jnp.float32))
        out_ref[pl.ds(block, 1), :] = jnp.sum(sums, axis=0, keepdims=True)
        return carry

    lax.fori_loop(0, turns, one_block, 0)


def column_norms(stride, info, shift, weight, place, root):
    work = shift.shape[0] * place.size
    return pl.pallas_call(
        functools.partial(norm_kernel, stride),
        out_shape=jax.ShapeDtypeStruct(place.shape, jnp.float32),
        in_specs=[spec(pltpu.SMEM)] + [spec(pltpu.VMEM)] * 4,
        out_specs=spec(pltpu.VMEM),
        cost_estimate=pl.CostEstimate(
            flops=3000 * work, bytes_accessed=8 * work, transcendentals=work
        ),
        compiler_params=pltpu.CompilerParams(vmem_limit_bytes=VMEM_LIMIT),
    )(info, shift, weight, place, root)


def apply_kernel(
    stride, info_ref, rows_ref, shift_ref, weight_ref, place_ref, root_ref, inverse_ref, out_ref
):
    live, half, blocks = info_ref[0], info_ref[1], info_ref[2]
    tiles = (live + POLE_TILE - 1) // POLE_TILE
    row_total = rows_ref.shape[0]
    width = place_ref.shape[1]
    turns = (blocks * LANE + width - 1) // width
    out_ref[...] = jnp.zeros(out_ref.shape, out_ref.dtype)

    def one_block(block, carry):
        offsets = offsets_from(place_ref[pl.ds(block, 1), :], stride, half)
        root = root_ref[pl.ds(block, 1), :]
        inverse = inverse_ref[pl.ds(block, 1), :]

        def one_tile(tile, running):
            opening = pl.multiple_of(tile * POLE_TILE, POLE_TILE)
            pieces = []
            for part in range(POLE_TILE // PART):
                term = quotients(
                    opening + part * PART, stride, offsets, shift_ref, weight_ref, root
                )
                pieces.append((term * inverse).astype(jnp.bfloat16))
            return running + jnp.dot(
                rows_ref[:, pl.ds(opening, POLE_TILE)],
                jnp.concatenate(pieces, axis=0),
                preferred_element_type=jnp.float32,
            )

        total = lax.fori_loop(0, tiles, one_tile, jnp.zeros((row_total, width), jnp.float32))
        out_ref[:, pl.ds(pl.multiple_of(block * width, width), width)] = total.astype(
            out_ref.dtype
        )
        return carry

    lax.fori_loop(0, turns, one_block, 0)


def cauchy_product(stride, info, rows, shift, weight, place, root, inverse):
    return pl.pallas_call(
        functools.partial(apply_kernel, stride),
        out_shape=jax.ShapeDtypeStruct((rows.shape[0], place.size), jnp.bfloat16),
        in_specs=[spec(pltpu.SMEM)] + [spec(pltpu.VMEM)] * 6,
        out_specs=spec(pltpu.VMEM),
        cost_estimate=pl.CostEstimate(
            flops=3000 * shift.shape[0] * place.size, bytes_accessed=0, transcendentals=0
        ),
        compiler_params=pltpu.CompilerParams(vmem_limit_bytes=VMEM_LIMIT),
    )(info, rows, shift, weight, place, root, inverse)


def ceil_to(value, unit):
    return (value + unit - 1) // unit * unit


def own_blocks(values, group, member):
    spread = values.reshape(-1, group, LANE)
    return lax.dynamic_index_in_dim(spread, member, 1, keepdims=False)


def block_share(live, group, member):
    total = (live + LANE - 1) // LANE
    return jnp.maximum((total - member + group - 1) // group, 0)


def greet(devices):
    barrier = pltpu.get_barrier_semaphore()
    for device in devices:
        pl.semaphore_signal(barrier, inc=1, device_id=device, device_id_type=MESH)
    pl.semaphore_wait(barrier, len(devices))


def scatter_kernel(row_count, col_count, source_ref, out_ref, send_sem, recv_sem, own_sem):
    merge = lax.axis_index("merge")
    row, col = lax.axis_index("row"), lax.axis_index("col")
    group = row_count * col_count
    me = row * col_count + col
    others = []
    for k in range(1, group):
        peer = lax.rem(me + k, group)
        others.append((merge, peer // col_count, lax.rem(peer, col_count)))
    greet(others)
    copies = []
    for k, device in enumerate(others):
        copy = pltpu.make_async_remote_copy(
            src_ref=source_ref.at[device[1]],
            dst_ref=out_ref.at[me],
            send_sem=send_sem.at[k],
            recv_sem=recv_sem.at[k],
            device_id=device,
            device_id_type=MESH,
        )
        copy.start()
        copies.append(copy)
    own = pltpu.make_async_copy(source_ref.at[row], out_ref.at[me], own_sem)
    own.start()
    own.wait()
    for copy in copies:
        copy.wait()


def gather_kernel(row_count, col_count, source_ref, out_ref, send_sem, recv_sem, own_sem):
    merge = lax.axis_index("merge")
    row, col = lax.axis_index("row"), lax.axis_index("col")
    rows, width = source_ref.shape
    parity = lax.rem(row, 2)
    mate = (merge, row + 1 - 2 * parity, col)
    count = row_count // 2 * col_count
    me = row // 2 * col_count + col

    def device_of(index):
        return (merge, index // col_count * 2 + parity, lax.rem(index, col_count))

    def place_of(device):
        return out_ref.at[
            pl.ds(pl.multiple_of(device[1] * rows, rows), rows),
            pl.ds(pl.multiple_of(device[2] * width, width), width),
        ]

    def send(source, target, device, number):
        copy = pltpu.make_async_remote_copy(
            src_ref=source,
            dst_ref=target,
            send_sem=send_sem.at[number],
            recv_sem=recv_sem.at[number],
            device_id=device,
            device_id_type=MESH,
        )
        copy.start()
        return copy

    others = [device_of(lax.rem(me + k, count)) for k in range(1, count)]
    greet(others + [mate])
    mine = place_of((merge, row, col))
    far = [send(source_ref, mine, device, k) for k, device in enumerate(others)]
    near = [send(source_ref, mine, mate, count - 1)]
    own = pltpu.make_async_copy(source_ref, mine, own_sem)
    own.start()
    for k, copy in enumerate(far):
        copy.wait_recv()
        piece = place_of(device_of(lax.rem(me - (k + 1) + count, count)))
        near.append(send(piece, piece, mate, count + k))
    own.wait()
    for copy in far:
        copy.wait_send()
    for copy in near:
        copy.wait()


def exchange(source, gathers, number):
    row_count, col_count = lax.axis_size("row"), lax.axis_size("col")
    group = row_count * col_count
    rows, width = source.shape[-2:]
    shape = (row_count * rows, col_count * width) if gathers else (group, rows, width)
    return pl.pallas_call(
        functools.partial(
            gather_kernel if gathers else scatter_kernel, row_count, col_count
        ),
        out_shape=jax.ShapeDtypeStruct(shape, source.dtype),
        in_specs=[spec(pl.ANY)],
        out_specs=spec(pl.ANY),
        scratch_shapes=[
            pltpu.SemaphoreType.DMA((group - 1,)),
            pltpu.SemaphoreType.DMA((group - 1,)),
            pltpu.SemaphoreType.DMA,
        ],
        compiler_params=pltpu.CompilerParams(collective_id=number, has_side_effects=True),
    )(source)


def join_columns(piece, number):
    row_count = lax.axis_size("row")
    return exchange(piece.reshape(row_count, -1, piece.shape[1]), False, number)


def spread_moved(moved):
    col_count, col_index = lax.axis_size("col"), lax.axis_index("col")
    rows, width = moved.shape[1], col_count * moved.shape[2]
    pieces = jnp.zeros(moved.shape, moved.dtype)
    for k in range(col_count):
        part = lax.dynamic_index_in_dim(moved, (col_index + k) % col_count, 0, keepdims=False)
        if k:
            pairs = [(c, (c + k) % col_count) for c in range(col_count)]
            part = lax.ppermute(part, "col", pairs)
        pieces = lax.dynamic_update_index_in_dim(
            pieces, part, (col_index - k + col_count) % col_count, 0
        )
    pieces = pieces.reshape(col_count, rows, -1, LANE)
    return jnp.transpose(pieces, (1, 2, 0, 3)).reshape(rows, width)


def spread_poles(values, live, limit, masked):
    values = values[:limit]
    if masked:
        values = jnp.where(jnp.arange(limit, dtype=jnp.int32) < live, values, 0.0)
    return jnp.broadcast_to(values[:, None], (limit, LANE))


def shards(
    eigen_rows,
    live_one,
    order_one,
    poles_one,
    weights_one,
    roots_one,
    live_two,
    order_two,
    poles_two,
    weights_two,
    roots_two,
):
    col_count, row_count = lax.axis_size("col"), lax.axis_size("row")
    col_index, row_index = lax.axis_index("col"), lax.axis_index("row")
    merge_index = lax.axis_index("merge")
    merge_order = order_one.shape[1]
    group, member = row_count * col_count, row_index * col_count + col_index
    most = 3 * merge_order // 8
    pole_limit = ceil_to(most, max(POLE_TILE, LANE * col_count))
    share = pole_limit // col_count
    wide_one = ceil_to(most, LANE * group)
    wide_two = ceil_to(2 * most, LANE * group)
    out_width = 2 * merge_order // col_count
    zero = jnp.zeros((), jnp.int32)

    half = merge_index % 2
    pair_first = merge_index - half
    count_first, count_second = live_two[pair_first], live_two[pair_first + 1]
    count_own = live_two[merge_index]
    joined = count_first + count_second
    pairs = [(k, k ^ 1) for k in range(lax.axis_size("merge"))]
    own_roots = roots_two[0, :most]
    other_roots = lax.ppermute(own_roots, "merge", pairs)
    roots_first = jnp.where(half == 0, own_roots, other_roots)
    roots_second = jnp.where(half == 0, other_roots, own_roots)
    columns = jnp.arange(wide_two, dtype=jnp.int32)
    from_first = columns < count_first
    padded_first = jnp.concatenate([roots_first, jnp.zeros((wide_two - most,), jnp.float32)])
    padded_second = jnp.concatenate(
        [jnp.zeros((most,), jnp.float32), roots_second, jnp.zeros((wide_two,), jnp.float32)]
    )
    moved_second = lax.dynamic_slice_in_dim(padded_second, most - count_first, wide_two)
    root_shift = jnp.where(from_first, padded_first, moved_second)
    root_shift = jnp.where(columns < joined, root_shift, 0.5)
    root_place = jnp.where(from_first, 2 * columns, 2 * (columns - count_first) + 1)
    root_place = wide_columns(own_blocks(root_place.astype(jnp.float32), group, member))
    root_shift = wide_columns(own_blocks(root_shift, group, member))
    blocks_two = block_share(joined, group, member)
    info_two = jnp.stack([count_own, half, blocks_two]).astype(jnp.int32)
    shift_two = spread_poles(poles_two[0], count_own, pole_limit, False)
    weight_two = spread_poles(weights_two[0], count_own, pole_limit, True)
    sums_two = column_norms(2, info_two, shift_two, weight_two, root_place, root_shift)
    sums_two = sums_two + lax.ppermute(sums_two, "merge", pairs)

    live = live_one[merge_index]
    first = col_index * share
    gathered = lax.all_gather(eigen_rows[0], "col", axis=1, tiled=True)
    column_one = jnp.arange(wide_one, dtype=jnp.int32).astype(jnp.float32)
    place_one = wide_columns(own_blocks(column_one, group, member))
    root_one = wide_columns(own_blocks(roots_one[0, :wide_one], group, member))
    info_one = jnp.stack([live, zero, block_share(live, group, member)]).astype(jnp.int32)
    shift_one = spread_poles(poles_one[0], live, pole_limit, False)
    weight_one = spread_poles(weights_one[0], live, pole_limit, True)
    sums_one = column_norms(1, info_one, shift_one, weight_one, place_one, root_one)
    inverse_one = 1.0 / jnp.sqrt(sums_one)
    inverse_two = 1.0 / jnp.sqrt(sums_two)
    gathered, inverse_one, inverse_two, weight_one, weight_two = lax.optimization_barrier(
        (gathered, inverse_one, inverse_two, weight_one, weight_two)
    )
    picked, table = pick_one(jnp.stack([first, live]).astype(jnp.int32), order_one[0], gathered, share)
    rows_one = exchange(picked, True, 0)
    level = cauchy_product(
        1, info_one, rows_one, shift_one, weight_one, place_one, root_one, inverse_one
    )
    level = join_columns(level, 1)

    slots = jnp.arange(merge_order, dtype=jnp.int32)
    slot_block = slots // LANE
    level_place = (slot_block % group * (wide_one // group // LANE) + slot_block // group) * LANE
    place = jnp.where(slots < live, level_place + slots % LANE, wide_one + order_one[0])
    offset = jnp.where(half == 0, -count_second, -merge_order)
    low = jnp.where(half == 0, joined, merge_order + count_second)
    high = jnp.where(half == 0, merge_order + count_second, 2 * merge_order)
    low_block, high_block = low // LANE, (high + LANE - 1) // LANE
    low_turn = (low_block - col_index + col_count - 1) // col_count
    high_turn = (high_block - col_index + col_count - 1) // col_count
    info_pick = jnp.stack(
        [first, count_own, offset + col_index * LANE, low_turn, high_turn]
    ).astype(jnp.int32)
    order_pad = jnp.pad(order_two[0], (0, LANE))
    moved_shape = (col_count, gathered.shape[0], out_width // col_count)
    picked, moved = pick_two(
        col_count * LANE, info_pick, order_pad, place, level, table, share, moved_shape
    )
    rows_two = exchange(picked, True, 2)
    rows_two, moved = lax.optimization_barrier((rows_two, moved))
    mixed = cauchy_product(
        2,
        info_two,
        rows_two,
        shift_two,
        weight_two,
        root_place,
        root_shift,
        inverse_two,
    )
    mixed = join_columns(mixed, 3)
    rows = mixed.shape[1]
    mixed = mixed.reshape(group, rows, -1, LANE)
    mixed = jnp.transpose(mixed, (1, 2, 0, 3)).reshape(rows, wide_two)
    mixed = jnp.pad(mixed, ((0, 0), (0, 2 * merge_order - wide_two)))
    begin = col_index * out_width
    mixed = lax.dynamic_slice_in_dim(mixed, begin, out_width, 1)
    own = jnp.arange(out_width, dtype=jnp.int32) + begin
    keep = (own >= low) & (own < high)
    moved = jnp.where(keep[None, :], spread_moved(moved), jnp.zeros((), jnp.bfloat16))
    result = jnp.where((own < joined)[None, :], mixed, moved)
    return result[None]


def solution(mesh):
    placed = (
        P("merge", "row", "col"),
        P(),
        P("merge", None),
        P("merge", None),
        P("merge", None),
        P("merge", None),
        P(),
        P("merge", None),
        P("merge", None),
        P("merge", None),
        P("merge", None),
    )
    return jax.shard_map(
        shards, mesh=mesh, in_specs=placed, out_specs=P("merge", "row", "col"), check_vma=False
    )
```

```python
import functools

import jax
import jax.numpy as jnp
from jax import lax
from jax.experimental import pallas as pl
from jax.experimental.pallas import tpu as pltpu
from jax.sharding import PartitionSpec as P

LANE = 128
PART = 32
POLE_TILE = 1024
VMEM_LIMIT = 56 * 1024 * 1024
MESH = pl.DeviceIdType.MESH


def inverse_of(distance):
    guess = pl.reciprocal(distance, approx=True)
    return guess * (2.0 - distance * guess)


def spec(space):
    return pl.BlockSpec(memory_space=space)


def fill_table(source_ref, table_ref, start=0):
    rows, width = source_ref.shape
    blocks = width // LANE
    unroll = max(k for k in (8, 6, 4, 3, 2, 1) if blocks % k == 0)

    def some(turn, carry):
        for k in range(unroll):
            opening = pl.multiple_of((turn * unroll + k) * LANE, LANE)
            block = source_ref[:, pl.ds(opening, LANE)].astype(jnp.float32)
            table_ref[pl.ds(start + opening, LANE), 0:rows] = block.T
        return carry

    lax.fori_loop(0, blocks // unroll, some, 0)


def pick_block(table_ref, stage_ref, index_of, rows):
    for k in range(LANE):
        stage_ref[k : k + 1, :] = table_ref[pl.ds(index_of(k), 1), :]
    return stage_ref[...].T[0:rows, :].astype(jnp.bfloat16)


def pick_one_kernel(info_ref, order_ref, source_ref, out_ref, table_ref, stage_ref):
    rows = source_ref.shape[0]
    table_ref[...] = jnp.zeros(table_ref.shape, jnp.float32)
    fill_table(source_ref, table_ref)
    out_ref[...] = jnp.zeros(out_ref.shape, out_ref.dtype)
    first, live = info_ref[0], info_ref[1]
    count = jnp.clip((live - first + LANE - 1) // LANE, 0, out_ref.shape[1] // LANE)

    def one(step, carry):
        opening = pl.multiple_of(step * LANE, LANE)
        out_ref[:, pl.ds(opening, LANE)] = pick_block(
            table_ref, stage_ref, lambda k: order_ref[first + opening + k], rows
        )
        return carry

    lax.fori_loop(0, count, one, 0)


def pick_one(info, order, source, width):
    rows, total = source.shape
    return pl.pallas_call(
        pick_one_kernel,
        out_shape=(
            jax.ShapeDtypeStruct((rows, width), jnp.bfloat16),
            jax.ShapeDtypeStruct((total, LANE), jnp.float32),
        ),
        in_specs=[spec(pltpu.SMEM), spec(pltpu.SMEM), spec(pltpu.VMEM)],
        out_specs=(spec(pltpu.VMEM), spec(pltpu.VMEM)),
        scratch_shapes=[pltpu.VMEM((LANE, LANE), jnp.float32)],
        compiler_params=pltpu.CompilerParams(vmem_limit_bytes=VMEM_LIMIT),
    )(info, order, source)


def pick_two_kernel(
    stride,
    info_ref,
    order_ref,
    place_ref,
    level_ref,
    source_ref,
    out_ref,
    moved_ref,
    table_ref,
    stage_ref,
    copy_sem,
):
    group, rows, width = level_ref.shape
    wide = group * width
    copy = pltpu.make_async_copy(
        source_ref, table_ref.at[pl.ds(wide, source_ref.shape[0])], copy_sem
    )
    copy.start()
    out_ref[...] = jnp.zeros(out_ref.shape, out_ref.dtype)
    moved_ref[...] = jnp.zeros(moved_ref.shape, moved_ref.dtype)
    table_ref[0:wide, :] = jnp.zeros((wide, LANE), jnp.float32)
    for part in range(group):
        fill_table(level_ref.at[part], table_ref, part * width)
    copy.wait()
    first, live = info_ref[0], info_ref[1]
    count = jnp.clip((live - first + LANE - 1) // LANE, 0, out_ref.shape[1] // LANE)

    def one(step, carry):
        opening = pl.multiple_of(step * LANE, LANE)
        out_ref[:, pl.ds(opening, LANE)] = pick_block(
            table_ref, stage_ref, lambda k: place_ref[order_ref[first + opening + k]], rows
        )
        return carry

    lax.fori_loop(0, count, one, 0)
    offset, low, high = info_ref[2], info_ref[3], info_ref[4]

    per_part = moved_ref.shape[2] // LANE

    def other(step, carry):
        opening = pl.multiple_of(lax.rem(step, per_part) * LANE, LANE)
        begin = offset + step * stride
        moved_ref[step // per_part, :, pl.ds(opening, LANE)] = pick_block(
            table_ref, stage_ref, lambda k: place_ref[order_ref[begin + k]], rows
        )
        return carry

    lax.fori_loop(low, high, other, 0)


def pick_two(stride, info, order, place, level, table, width, moved_shape):
    group, rows, wide = level.shape
    wide = wide * group
    return pl.pallas_call(
        functools.partial(pick_two_kernel, stride),
        out_shape=(
            jax.ShapeDtypeStruct((rows, width), jnp.bfloat16),
            jax.ShapeDtypeStruct(moved_shape, jnp.bfloat16),
        ),
        in_specs=[spec(pltpu.SMEM)] * 3 + [spec(pltpu.VMEM), spec(pl.ANY)],
        out_specs=(spec(pltpu.VMEM), spec(pltpu.VMEM)),
        scratch_shapes=[
            pltpu.VMEM((table.shape[0] + wide, LANE), jnp.float32),
            pltpu.VMEM((LANE, LANE), jnp.float32),
            pltpu.SemaphoreType.DMA,
        ],
        compiler_params=pltpu.CompilerParams(vmem_limit_bytes=VMEM_LIMIT),
    )(info, order, place, level, table)


def wide_columns(values):
    width = 2 * LANE if values.shape[0] % 2 == 0 else LANE
    return values.reshape(-1, width)


def across(values, width):
    return jnp.concatenate([values] * (width // LANE), axis=1)


def offsets_from(place, stride, half):
    steps = lax.broadcasted_iota(jnp.int32, (PART, place.shape[1]), 0) * stride + half
    return steps.astype(jnp.float32) - place


def quotients(start, stride, offsets, shift_ref, weight_ref, root):
    width = root.shape[1]
    shifts = across(shift_ref[pl.ds(start, PART), :], width)
    distance = (offsets + (start * stride).astype(jnp.float32)) + (shifts - root)
    return across(weight_ref[pl.ds(start, PART), :], width) * inverse_of(distance)


def norm_kernel(stride, info_ref, shift_ref, weight_ref, place_ref, root_ref, out_ref):
    live, half, blocks = info_ref[0], info_ref[1], info_ref[2]
    tiles = (live + POLE_TILE - 1) // POLE_TILE
    width = place_ref.shape[1]
    turns = (blocks * LANE + width - 1) // width
    out_ref[...] = jnp.ones(out_ref.shape, jnp.float32)

    def one_block(block, carry):
        offsets = offsets_from(place_ref[pl.ds(block, 1), :], stride, half)
        root = root_ref[pl.ds(block, 1), :]

        def one_tile(tile, running):
            opening = pl.multiple_of(tile * POLE_TILE, POLE_TILE)
            for part in range(POLE_TILE // PART):
                term = quotients(
                    opening + part * PART, stride, offsets, shift_ref, weight_ref, root
                )
                running = running + jnp.sum((term * term).reshape(PART // 8, 8, width), axis=0)
            return running

        sums = lax.fori_loop(0, tiles, one_tile, jnp.zeros((8, width), jnp.float32))
        out_ref[pl.ds(block, 1), :] = jnp.sum(sums, axis=0, keepdims=True)
        return carry

    lax.fori_loop(0, turns, one_block, 0)


def column_norms(stride, info, shift, weight, place, root):
    work = shift.shape[0] * place.size
    return pl.pallas_call(
        functools.partial(norm_kernel, stride),
        out_shape=jax.ShapeDtypeStruct(place.shape, jnp.float32),
        in_specs=[spec(pltpu.SMEM)] + [spec(pltpu.VMEM)] * 4,
        out_specs=spec(pltpu.VMEM),
        cost_estimate=pl.CostEstimate(
            flops=3000 * work, bytes_accessed=8 * work, transcendentals=work
        ),
        compiler_params=pltpu.CompilerParams(vmem_limit_bytes=VMEM_LIMIT),
    )(info, shift, weight, place, root)


def apply_kernel(
    stride, info_ref, rows_ref, shift_ref, weight_ref, place_ref, root_ref, inverse_ref, out_ref
):
    live, half, blocks = info_ref[0], info_ref[1], info_ref[2]
    tiles = (live + POLE_TILE - 1) // POLE_TILE
    row_total = rows_ref.shape[0]
    width = place_ref.shape[1]
    turns = (blocks * LANE + width - 1) // width
    out_ref[...] = jnp.zeros(out_ref.shape, out_ref.dtype)

    def one_block(block, carry):
        offsets = offsets_from(place_ref[pl.ds(block, 1), :], stride, half)
        root = root_ref[pl.ds(block, 1), :]
        inverse = inverse_ref[pl.ds(block, 1), :]

        def one_tile(tile, running):
            opening = pl.multiple_of(tile * POLE_TILE, POLE_TILE)
            pieces = []
            for part in range(POLE_TILE // PART):
                term = quotients(
                    opening + part * PART, stride, offsets, shift_ref, weight_ref, root
                )
                pieces.append((term * inverse).astype(jnp.bfloat16))
            return running + jnp.dot(
                rows_ref[:, pl.ds(opening, POLE_TILE)],
                jnp.concatenate(pieces, axis=0),
                preferred_element_type=jnp.float32,
            )

        total = lax.fori_loop(0, tiles, one_tile, jnp.zeros((row_total, width), jnp.float32))
        out_ref[:, pl.ds(pl.multiple_of(block * width, width), width)] = total.astype(
            out_ref.dtype
        )
        return carry

    lax.fori_loop(0, turns, one_block, 0)


def cauchy_product(stride, info, rows, shift, weight, place, root, inverse):
    return pl.pallas_call(
        functools.partial(apply_kernel, stride),
        out_shape=jax.ShapeDtypeStruct((rows.shape[0], place.size), jnp.bfloat16),
        in_specs=[spec(pltpu.SMEM)] + [spec(pltpu.VMEM)] * 6,
        out_specs=spec(pltpu.VMEM),
        cost_estimate=pl.CostEstimate(
            flops=3000 * shift.shape[0] * place.size, bytes_accessed=0, transcendentals=0
        ),
        compiler_params=pltpu.CompilerParams(vmem_limit_bytes=VMEM_LIMIT),
    )(info, rows, shift, weight, place, root, inverse)


def ceil_to(value, unit):
    return (value + unit - 1) // unit * unit


def own_blocks(values, group, member):
    spread = values.reshape(-1, group, LANE)
    return lax.dynamic_index_in_dim(spread, member, 1, keepdims=False)


def block_share(live, group, member):
    total = (live + LANE - 1) // LANE
    return jnp.maximum((total - member + group - 1) // group, 0)


def greet(devices):
    barrier = pltpu.get_barrier_semaphore()
    for device in devices:
        pl.semaphore_signal(barrier, inc=1, device_id=device, device_id_type=MESH)
    pl.semaphore_wait(barrier, len(devices))


def scatter_kernel(row_count, col_count, source_ref, out_ref, send_sem, recv_sem, own_sem):
    merge = lax.axis_index("merge")
    row, col = lax.axis_index("row"), lax.axis_index("col")
    group = row_count * col_count
    me = row * col_count + col
    others = []
    for k in range(1, group):
        peer = lax.rem(me + k, group)
        others.append((merge, peer // col_count, lax.rem(peer, col_count)))
    greet(others)
    copies = []
    for k, device in enumerate(others):
        copy = pltpu.make_async_remote_copy(
            src_ref=source_ref.at[device[1]],
            dst_ref=out_ref.at[me],
            send_sem=send_sem.at[k],
            recv_sem=recv_sem.at[k],
            device_id=device,
            device_id_type=MESH,
        )
        copy.start()
        copies.append(copy)
    own = pltpu.make_async_copy(source_ref.at[row], out_ref.at[me], own_sem)
    own.start()
    own.wait()
    for copy in copies:
        copy.wait()


def gather_kernel(row_count, col_count, source_ref, out_ref, send_sem, recv_sem, own_sem):
    merge = lax.axis_index("merge")
    row, col = lax.axis_index("row"), lax.axis_index("col")
    rows, width = source_ref.shape
    parity = lax.rem(row, 2)
    mate = (merge, row + 1 - 2 * parity, col)
    count = row_count // 2 * col_count
    me = row // 2 * col_count + col

    def device_of(index):
        return (merge, index // col_count * 2 + parity, lax.rem(index, col_count))

    def place_of(device):
        return out_ref.at[
            pl.ds(pl.multiple_of(device[1] * rows, rows), rows),
            pl.ds(pl.multiple_of(device[2] * width, width), width),
        ]

    def send(source, target, device, number):
        copy = pltpu.make_async_remote_copy(
            src_ref=source,
            dst_ref=target,
            send_sem=send_sem.at[number],
            recv_sem=recv_sem.at[number],
            device_id=device,
            device_id_type=MESH,
        )
        copy.start()
        return copy

    others = [device_of(lax.rem(me + k, count)) for k in range(1, count)]
    greet(others + [mate])
    mine = place_of((merge, row, col))
    far = [send(source_ref, mine, device, k) for k, device in enumerate(others)]
    near = [send(source_ref, mine, mate, count - 1)]
    own = pltpu.make_async_copy(source_ref, mine, own_sem)
    own.start()
    for k, copy in enumerate(far):
        copy.wait_recv()
        piece = place_of(device_of(lax.rem(me - (k + 1) + count, count)))
        near.append(send(piece, piece, mate, count + k))
    own.wait()
    for copy in far:
        copy.wait_send()
    for copy in near:
        copy.wait()


def exchange(source, gathers, number):
    row_count, col_count = lax.axis_size("row"), lax.axis_size("col")
    group = row_count * col_count
    rows, width = source.shape[-2:]
    shape = (row_count * rows, col_count * width) if gathers else (group, rows, width)
    return pl.pallas_call(
        functools.partial(
            gather_kernel if gathers else scatter_kernel, row_count, col_count
        ),
        out_shape=jax.ShapeDtypeStruct(shape, source.dtype),
        in_specs=[spec(pl.ANY)],
        out_specs=spec(pl.ANY),
        scratch_shapes=[
            pltpu.SemaphoreType.DMA((group - 1,)),
            pltpu.SemaphoreType.DMA((group - 1,)),
            pltpu.SemaphoreType.DMA,
        ],
        compiler_params=pltpu.CompilerParams(collective_id=number, has_side_effects=True),
    )(source)


def join_rows(piece):
    rows, width = piece.shape
    row_count, col_count = lax.axis_size("row"), lax.axis_size("col")
    parts = lax.all_gather(piece, ("row", "col"), axis=0, tiled=False)
    parts = parts.reshape(row_count, col_count, rows, width)
    return jnp.transpose(parts, (0, 2, 1, 3)).reshape(row_count * rows, col_count * width)


def join_columns(piece, number):
    row_count = lax.axis_size("row")
    return exchange(piece.reshape(row_count, -1, piece.shape[1]), False, number)


def spread_moved(moved):
    col_count, col_index = lax.axis_size("col"), lax.axis_index("col")
    rows, width = moved.shape[1], col_count * moved.shape[2]
    pieces = jnp.zeros(moved.shape, moved.dtype)
    for k in range(col_count):
        part = lax.dynamic_index_in_dim(moved, (col_index + k) % col_count, 0, keepdims=False)
        if k:
            pairs = [(c, (c + k) % col_count) for c in range(col_count)]
            part = lax.ppermute(part, "col", pairs)
        pieces = lax.dynamic_update_index_in_dim(
            pieces, part, (col_index - k + col_count) % col_count, 0
        )
    pieces = pieces.reshape(col_count, rows, -1, LANE)
    return jnp.transpose(pieces, (1, 2, 0, 3)).reshape(rows, width)


def spread_poles(values, live, limit, masked):
    values = values[:limit]
    if masked:
        values = jnp.where(jnp.arange(limit, dtype=jnp.int32) < live, values, 0.0)
    return jnp.broadcast_to(values[:, None], (limit, LANE))


def shards(
    eigen_rows,
    live_one,
    order_one,
    poles_one,
    weights_one,
    roots_one,
    live_two,
    order_two,
    poles_two,
    weights_two,
    roots_two,
):
    col_count, row_count = lax.axis_size("col"), lax.axis_size("row")
    col_index, row_index = lax.axis_index("col"), lax.axis_index("row")
    merge_index = lax.axis_index("merge")
    merge_order = order_one.shape[1]
    group, member = row_count * col_count, row_index * col_count + col_index
    most = 3 * merge_order // 8
    pole_limit = ceil_to(most, max(POLE_TILE, LANE * col_count))
    share = pole_limit // col_count
    wide_one = ceil_to(most, LANE * group)
    wide_two = ceil_to(2 * most, LANE * group)
    out_width = 2 * merge_order // col_count
    zero = jnp.zeros((), jnp.int32)

    half = merge_index % 2
    pair_first = merge_index - half
    count_first, count_second = live_two[pair_first], live_two[pair_first + 1]
    count_own = live_two[merge_index]
    joined = count_first + count_second
    pairs = [(k, k ^ 1) for k in range(lax.axis_size("merge"))]
    own_roots = roots_two[0, :most]
    other_roots = lax.ppermute(own_roots, "merge", pairs)
    roots_first = jnp.where(half == 0, own_roots, other_roots)
    roots_second = jnp.where(half == 0, other_roots, own_roots)
    columns = jnp.arange(wide_two, dtype=jnp.int32)
    from_first = columns < count_first
    padded_first = jnp.concatenate([roots_first, jnp.zeros((wide_two - most,), jnp.float32)])
    padded_second = jnp.concatenate(
        [jnp.zeros((most,), jnp.float32), roots_second, jnp.zeros((wide_two,), jnp.float32)]
    )
    moved_second = lax.dynamic_slice_in_dim(padded_second, most - count_first, wide_two)
    root_shift = jnp.where(from_first, padded_first, moved_second)
    root_shift = jnp.where(columns < joined, root_shift, 0.5)
    root_place = jnp.where(from_first, 2 * columns, 2 * (columns - count_first) + 1)
    root_place = wide_columns(own_blocks(root_place.astype(jnp.float32), group, member))
    root_shift = wide_columns(own_blocks(root_shift, group, member))
    blocks_two = block_share(joined, group, member)
    info_two = jnp.stack([count_own, half, blocks_two]).astype(jnp.int32)
    shift_two = spread_poles(poles_two[0], count_own, pole_limit, False)
    weight_two = spread_poles(weights_two[0], count_own, pole_limit, True)
    sums_two = column_norms(2, info_two, shift_two, weight_two, root_place, root_shift)
    sums_two = sums_two + lax.ppermute(sums_two, "merge", pairs)

    live = live_one[merge_index]
    first = col_index * share
    gathered = lax.all_gather(eigen_rows[0], "col", axis=1, tiled=True)
    column_one = jnp.arange(wide_one, dtype=jnp.int32).astype(jnp.float32)
    place_one = wide_columns(own_blocks(column_one, group, member))
    root_one = wide_columns(own_blocks(roots_one[0, :wide_one], group, member))
    info_one = jnp.stack([live, zero, block_share(live, group, member)]).astype(jnp.int32)
    shift_one = spread_poles(poles_one[0], live, pole_limit, False)
    weight_one = spread_poles(weights_one[0], live, pole_limit, True)
    sums_one = column_norms(1, info_one, shift_one, weight_one, place_one, root_one)
    inverse_one = 1.0 / jnp.sqrt(sums_one)
    inverse_two = 1.0 / jnp.sqrt(sums_two)
    gathered, inverse_one, weight_one = lax.optimization_barrier(
        (gathered, inverse_one, weight_one)
    )
    picked, table = pick_one(jnp.stack([first, live]).astype(jnp.int32), order_one[0], gathered, share)
    rows_one = join_rows(picked)
    rows_one, inverse_two, weight_two = lax.optimization_barrier(
        (rows_one, inverse_two, weight_two)
    )
    level = cauchy_product(
        1, info_one, rows_one, shift_one, weight_one, place_one, root_one, inverse_one
    )
    level = join_columns(level, 1)

    slots = jnp.arange(merge_order, dtype=jnp.int32)
    slot_block = slots // LANE
    level_place = (slot_block % group * (wide_one // group // LANE) + slot_block // group) * LANE
    place = jnp.where(slots < live, level_place + slots % LANE, wide_one + order_one[0])
    offset = jnp.where(half == 0, -count_second, -merge_order)
    low = jnp.where(half == 0, joined, merge_order + count_second)
    high = jnp.where(half == 0, merge_order + count_second, 2 * merge_order)
    low_block, high_block = low // LANE, (high + LANE - 1) // LANE
    low_turn = (low_block - col_index + col_count - 1) // col_count
    high_turn = (high_block - col_index + col_count - 1) // col_count
    info_pick = jnp.stack(
        [first, count_own, offset + col_index * LANE, low_turn, high_turn]
    ).astype(jnp.int32)
    order_pad = jnp.pad(order_two[0], (0, LANE))
    moved_shape = (col_count, gathered.shape[0], out_width // col_count)
    picked, moved = pick_two(
        col_count * LANE, info_pick, order_pad, place, level, table, share, moved_shape
    )
    rows_two = exchange(picked, True, 2)
    rows_two, moved = lax.optimization_barrier((rows_two, moved))
    mixed = cauchy_product(
        2,
        info_two,
        rows_two,
        shift_two,
        weight_two,
        root_place,
        root_shift,
        inverse_two,
    )
    mixed = join_columns(mixed, 3)
    rows = mixed.shape[1]
    mixed = mixed.reshape(group, rows, -1, LANE)
    mixed = jnp.transpose(mixed, (1, 2, 0, 3)).reshape(rows, wide_two)
    mixed = jnp.pad(mixed, ((0, 0), (0, 2 * merge_order - wide_two)))
    begin = col_index * out_width
    mixed = lax.dynamic_slice_in_dim(mixed, begin, out_width, 1)
    own = jnp.arange(out_width, dtype=jnp.int32) + begin
    keep = (own >= low) & (own < high)
    moved = jnp.where(keep[None, :], spread_moved(moved), jnp.zeros((), jnp.bfloat16))
    result = jnp.where((own < joined)[None, :], mixed, moved)
    return result[None]


def solution(mesh):
    placed = (
        P("merge", "row", "col"),
        P(),
        P("merge", None),
        P("merge", None),
        P("merge", None),
        P("merge", None),
        P(),
        P("merge", None),
        P("merge", None),
        P("merge", None),
        P("merge", None),
    )
    return jax.shard_map(
        shards, mesh=mesh, in_specs=placed, out_specs=P("merge", "row", "col"), check_vma=False
    )
```
